768 devices in a mesh: grp: 96 (over x, z, core), sub: 8 (over y).
Axes of the slice: x: 4, y: 8, z: 12, core: 2. Of those that a mesh axis runs over, the one named last changes fastest.
Arguments:
- ocean_state: bfloat16 [8, 3145728], P(None, ('grp', 'sub')), may hold values from -6 to 6
- ocean_area: float32 [3145728], P(('grp', 'sub')), may hold values from 0.3 to 3
- atm_flux: bfloat16 [12, 786432], P(None, ('grp', 'sub')), may hold values from -6 to 6
- atm_area: float32 [786432], P(('grp', 'sub')), may hold values from 0.3 to 3
- coupling: float32 [12, 8], replicated, may hold values from -2 to 2
- remap_weight: bfloat16 [6144, 12, 128, 128], P(('grp', 'sub')), may hold values from -0.21875 to 0.21875
- send_block: int32 [768, 3, 8, 6], P(('grp', 'sub')), may hold values from 0 to 31
- send_count: int32 [768, 3, 8], P(('grp', 'sub')), may hold values from 2 to 6, as said below
- link_slot: int32 [6144, 12], P(('grp', 'sub')), may hold values from 0 to 143, as said below
- link_count: int32 [6144], P(('grp', 'sub')), may hold values from 1 to 12, as said below
Outputs:
- state_on_atm: bfloat16 [8, 786432], P(None, ('grp', 'sub'))
- flux_on_ocean: bfloat16 [12, 3145728], P(None, ('grp', 'sub'))
- imbalance: float32 [12], replicated
The draws below stay inside these ranges and needn't reach their ends.
Inputs may be any that keep to these rules, and one draw needn't show every extreme that they name: `send_count`: every rank has one route with exactly 6 live slots. `link_slot`: the 12 slots of one atmosphere block differ, and each is a live slot of the sending route. `link_count`: every rank has an atmosphere block with all 12 links live.
All inputs are finite; a program needn't handle non-finite values.
Results may differ from the reference program's by a relative error of at most 0.0075.
Values may be sent and summed in bfloat16 or wider, within the bound.
No kernel may reach another device: no remote copies, remote signals or barrier semaphores. Data moves between devices by JAX's collectives and lax.ppermute only.
A program may use at most 32 MiB of HBM per device.

```python
import math
import jax
import jax.numpy as jnp
from jax import lax

FO = 8
FA = 12
BLK = 128
LINKS = 12
CAP = 6
OB = 32
AB = 8
OCELLS = 3145728
ACOLS = 786432
ABLOCKS = 6144
N_GRP = 96
N_SUB = 8


def route_counts(key):
    devices = N_GRP * N_SUB
    count_key = jax.random.fold_in(key, 101)
    base_counts = jax.random.randint(count_key, (devices, 3 * N_SUB), 2, CAP + 1)
    full_route = jax.random.randint(jax.random.fold_in(count_key, 1), (devices, 1), 0, 3 * N_SUB)
    route_ids = jnp.arange(3 * N_SUB, dtype=jnp.int32)[None, :]
    filled = jnp.where(route_ids == full_route, CAP, base_counts)
    return filled.reshape(devices, 3, N_SUB).astype(jnp.int32)


def draw_send_count(key, part):
    return route_counts(key)


def draw_link_slot(key, part):
    counts = route_counts(key)
    key = jax.random.fold_in(key, 7)
    devices = N_GRP * N_SUB
    slot_total = 3 * N_SUB * CAP
    rank_ids = jnp.arange(devices, dtype=jnp.int32)
    grp_of = rank_ids // N_SUB
    sub_of = rank_ids % N_SUB
    offsets = jnp.arange(3, dtype=jnp.int32)
    sub_ids = jnp.arange(N_SUB, dtype=jnp.int32)
    sources = (grp_of[:, None, None] + offsets[None, :, None] - 1) % N_GRP * N_SUB + sub_ids[None, None, :]
    row_ids = 2 - offsets
    got = counts[sources, row_ids[None, :, None], sub_of[:, None, None]]
    alive_slot = jnp.arange(CAP, dtype=jnp.int32)[None, None, None, :] < got[..., None]
    alive_slot = alive_slot.reshape(devices, 1, slot_total)
    scores = jax.random.randint(key, (devices, AB, slot_total), 0, 1 << 20) * slot_total + jnp.arange(slot_total, dtype=jnp.int32)
    scores = jnp.where(alive_slot, scores, -1)
    chosen = jax.lax.top_k(scores, LINKS)[1]
    return chosen.reshape(devices * AB, LINKS).astype(jnp.int32)


def draw_link_count(key, part):
    key = jax.random.fold_in(key, 13)
    devices = N_GRP * N_SUB
    base_counts = jax.random.randint(key, (devices, AB), 1, LINKS + 1)
    full_block = jax.random.randint(jax.random.fold_in(key, 1), (devices, 1), 0, AB)
    block_ids = jnp.arange(AB, dtype=jnp.int32)[None, :]
    return jnp.where(block_ids == full_block, LINKS, base_counts).reshape(devices * AB).astype(jnp.int32)


def with_ends(entries, key, smallest, largest):
    dims = entries.shape
    index_at = [jax.random.randint(jax.random.fold_in(key, axis), (), 0, dims[axis]) for axis in range(len(dims))]
    entries = entries.at[tuple(index_at)].set(smallest)
    longest = dims.index(max(dims))
    index_at[longest] = (index_at[longest] + 1) % dims[longest]
    return entries.at[tuple(index_at)].set(largest)


def shard_levels(own_key, shape, pieces, low, top_value):
    factor_of = 1.0
    for position, shards_of in pieces:
        steps = jax.random.uniform(jax.random.fold_in(jax.random.fold_in(own_key, 6), position), (shards_of,), jnp.float32, low / len(pieces), top_value / len(pieces))
        factor_of = factor_of * jnp.repeat(jnp.exp(steps), shape[position] // shards_of).reshape((-1,) + (1,) * (len(shape) - 1 - position))
    return factor_of


def noise(stream_key, dims, deviation, most, shards=(), kind=jnp.bfloat16):
    array = jax.random.normal(stream_key, dims, jnp.float32) * deviation
    if len(shards) > 0:
        array = shard_levels(stream_key, dims, shards, -0.22, 0.18) * array
    return jnp.clip(array, min=-most, max=most).astype(kind)


def setup_inputs(seed: int = 0) -> dict:
    keys = jax.random.split(jax.random.key(seed), 11)
    ocean_state = noise(keys[0], (FO, OCELLS), 1.0, 6.0, ((1, 768),))
    ocean_area = jnp.clip(jnp.exp(math.log(3.0) - 2.3025851 * jax.random.uniform(keys[1], (OCELLS,), jnp.float32) ** shard_levels(keys[1], (OCELLS,), ((0, 768),), -0.2, 0.2)), 0.3, 3.0)
    atm_flux = noise(keys[2], (FA, ACOLS), 1.0, 6.0, ((1, 768),))
    atm_area = jnp.clip(jnp.exp(math.log(3.0) - 2.3025851 * jax.random.uniform(keys[3], (ACOLS,), jnp.float32) ** shard_levels(keys[3], (ACOLS,), ((0, 768),), -0.2, 0.2)), 0.3, 3.0)
    coupling = noise(keys[4], (FA, FO), FO ** -0.5, 2.0, (), jnp.float32)
    remap_weight = noise(keys[5], (ABLOCKS, LINKS, BLK, BLK), (BLK * LINKS // 2) ** -0.5, 0.21875, ((0, 768),))
    send_block = with_ends(jax.random.randint(keys[6], (N_GRP * N_SUB, 3, N_SUB, CAP), 0, OB), jax.random.fold_in(keys[6], 1), 0, OB - 1).astype(jnp.int32)
    send_count = draw_send_count(jax.random.fold_in(keys[10], 71), 0)
    link_slot = draw_link_slot(jax.random.fold_in(keys[10], 71), 0)
    link_count = draw_link_count(jax.random.fold_in(keys[10], 71), 0)
    return {"ocean_state": ocean_state, "ocean_area": ocean_area, "atm_flux": atm_flux, "atm_area": atm_area, "coupling": coupling, "remap_weight": remap_weight, "send_block": send_block, "send_count": send_count, "link_slot": link_slot, "link_count": link_count}


def reference(ocean_state, ocean_area, atm_flux, atm_area, coupling, remap_weight, send_block, send_count, link_slot, link_count):
    devices = N_GRP * N_SUB
    slot_total = 3 * N_SUB * CAP
    blocks = ocean_state.reshape(FO, devices, OB, BLK)
    cap_ids = jnp.arange(CAP, dtype=jnp.int32)
    live_send = cap_ids[None, None, None, :] < send_count[:, :, :, None]
    rank_ids = jnp.arange(devices, dtype=jnp.int32)
    grp_of = rank_ids // N_SUB
    sub_of = rank_ids % N_SUB
    offsets = jnp.arange(3, dtype=jnp.int32)
    sub_ids = jnp.arange(N_SUB, dtype=jnp.int32)
    peers = (grp_of[:, None, None] + offsets[None, :, None] - 1) % N_GRP * N_SUB + sub_ids[None, None, :]
    row_ids = (2 - offsets).astype(jnp.int32)
    weights = remap_weight.reshape(devices, AB, LINKS, BLK, BLK)
    slot_of = link_slot.reshape(devices, AB, LINKS)
    used_of = jnp.arange(LINKS, dtype=jnp.int32)[None, None, :] < link_count.reshape(devices, AB)[:, :, None]
    fluxes = atm_flux.reshape(FA, devices, AB, BLK).transpose(1, 0, 2, 3)
    atm_areas = atm_area.reshape(devices, AB, BLK)

    def receive(inputs):
        peer_here, sub_here, weight, slot_ids, used_link, flux_here, area_here = inputs
        picked = send_block[peer_here[:, :, None], row_ids[:, None, None], sub_here, cap_ids[None, None, :]]
        alive_slot = live_send[peer_here[:, :, None], row_ids[:, None, None], sub_here, cap_ids[None, None, :]]
        arrived = blocks[:, peer_here[:, :, None], picked]
        arrived = jnp.where(alive_slot[None, :, :, :, None], arrived, jnp.zeros((), arrived.dtype)).reshape(FO, slot_total, BLK)
        taken = arrived[:, slot_ids]
        taken = jnp.where(used_link[None, :, :, None], taken, jnp.zeros((), taken.dtype))
        weight_wide = weight.astype(jnp.float32)
        state_sum = jnp.einsum('falr,alrq->faq', taken.astype(jnp.float32), weight_wide, precision=lax.Precision.HIGHEST)
        coupled = (flux_here.astype(jnp.float32) + jnp.einsum('gf,faq->gaq', coupling, state_sum, precision=lax.Precision.HIGHEST)).astype(jnp.bfloat16)
        link_part = jnp.einsum('gaq,alrq->algr', coupled.astype(jnp.float32), weight_wide, precision=lax.Precision.HIGHEST)
        link_part = jnp.where(used_link[:, :, None, None], link_part, jnp.zeros((), link_part.dtype))
        slot_part = jax.ops.segment_sum(link_part.reshape(AB * LINKS, FA, BLK), slot_ids.reshape(-1), num_segments=slot_total).astype(jnp.bfloat16)
        atm_part = lax.optimization_barrier(jnp.sum(area_here[None] * coupled.astype(jnp.float32), axis=(1, 2)))
        return (state_sum.astype(jnp.bfloat16), slot_part, atm_part)
    states, slot_parts, atm_parts = lax.map(receive, (peers, sub_of, weights, slot_of, used_of, fluxes, atm_areas))
    slot_parts = slot_parts.reshape(devices, 3, N_SUB, CAP, FA, BLK)
    ocean_areas = ocean_area.reshape(devices, OB, BLK)
    block_ids = jnp.arange(OB, dtype=jnp.int32)

    def collect(inputs):
        peer_here, sub_here, picks, alive_slot, area_here = inputs
        returned = slot_parts[peer_here[:, :, None], row_ids[:, None, None], sub_here, cap_ids[None, None, :]]
        block_hits = ((picks[..., None] == block_ids) & alive_slot[..., None]).reshape(slot_total, OB)
        block_hits = jnp.where(block_hits, 1.0, 0.0).astype(jnp.float32)
        flux_sum = jnp.einsum('sb,sgr->gbr', block_hits, returned.reshape(slot_total, FA, BLK).astype(jnp.float32), precision=lax.Precision.HIGHEST)
        return (flux_sum, lax.optimization_barrier(jnp.sum(area_here[None] * flux_sum, axis=(1, 2))))
    flux_parts, ocean_parts = lax.map(collect, (peers, sub_of, send_block, live_send, ocean_areas))
    state_on_atm = states.transpose(1, 0, 2, 3).reshape(FO, devices * AB * BLK)
    flux_on_ocean = flux_parts.transpose(1, 0, 2, 3).reshape(FA, devices * OB * BLK).astype(jnp.bfloat16)
    norm_scale = 1.0 / math.sqrt(devices * AB * BLK)
    imbalance = (lax.optimization_barrier(jnp.sum(atm_parts, axis=0)) - lax.optimization_barrier(jnp.sum(ocean_parts, axis=0))) * norm_scale
    return (state_on_atm, flux_on_ocean, imbalance)
```

```python
import functools
import math

import jax
import jax.numpy as jnp
from jax import lax
from jax.experimental import pallas as pl
from jax.experimental.pallas import tpu as pltpu
from jax.sharding import PartitionSpec as P

F32 = jnp.float32
BF16 = jnp.bfloat16
VMEM = pl.BlockSpec(memory_space=pltpu.VMEM)
SMEM = pl.BlockSpec(memory_space=pltpu.SMEM)
ANY = pl.BlockSpec(memory_space=pl.ANY)
LIMIT = 48 * 1024 * 1024


def gather_kernel(block_ref, state_ref, area_ref, out_ref, fields, high, low, rows):
    subs, offsets = out_ref.shape[0], out_ref.shape[1] // 64
    blocks = area_ref.shape[0]
    for b in range(blocks):
        fields[b] = state_ref[:, b * 128 : (b + 1) * 128].astype(F32)
    upper = area_ref[...].astype(BF16).astype(F32)
    high[...] = upper
    low[...] = area_ref[...] - upper
    rows[...] = jnp.zeros_like(rows)
    for o in range(offsets):
        for k in range(subs):
            for c in range(6):
                b = block_ref[o * 6 + c, 0, k]
                rows[o * subs + k, c : c + 1, :] = high[pl.ds(b, 1), :]
                rows[o * subs + k, 8 + c : 9 + c, :] = low[pl.ds(b, 1), :]
            for c in range(0, 6, 2):
                pair = [fields[block_ref[o * 6 + c + i, 0, k]] for i in range(2)]
                out_ref[k, o * 64 + c * 8 : o * 64 + c * 8 + 16, :] = jnp.concatenate(
                    pair, axis=0
                ).astype(BF16)
            out_ref[k, o * 64 + 48 : o * 64 + 64, :] = rows[o * subs + k].astype(BF16)


def middle_kernel(
    slot_ref,
    count_ref,
    own_ref,
    before_ref,
    after_ref,
    flux_ref,
    area_ref,
    coupling_ref,
    weight_hbm,
    state_out,
    before_out,
    own_out,
    after_out,
    total_out,
    weight,
    arrived,
    taken,
    state_sum,
    acc_low,
    acc_high,
    sems,
):
    blocks, links = weight_hbm.shape[0], weight_hbm.shape[1]
    subs = own_ref.shape[0]
    copies = [
        pltpu.make_async_copy(weight_hbm.at[a], weight.at[a], sems.at[a]) for a in range(blocks)
    ]
    for copy in copies:
        copy.start()
    for p, ref in enumerate((before_ref, own_ref, after_ref)):
        for j in range(subs):
            if p == 1:
                part = ref[j, 64:128, :]
            else:
                part = ref[j]
            arrived[(p * subs + j) * 8 : (p * subs + j + 1) * 8] = part.astype(F32).reshape(8, 8, 128)
    acc_low[...] = jnp.zeros_like(acc_low)
    acc_high[...] = jnp.zeros_like(acc_high)
    for a in range(blocks):
        live = count_ref[a]
        for link in range(links):
            slot = slot_ref[a, link]
            chunk = (slot * 171) >> 10
            tile = arrived[chunk * 2 + slot]
            taken[a, :, link * 128 : (link + 1) * 128] = jnp.where(link < live, tile, 0.0)
    for a in range(blocks):
        copies[a].wait()
        state_sum[:, a * 128 : (a + 1) * 128] = jnp.dot(
            taken[a].astype(BF16),
            weight[a].reshape(links * 128, 128),
            preferred_element_type=F32,
        )
    state = state_sum[...]
    state_out[...] = state.astype(BF16)
    flux = flux_ref[...].astype(F32)
    coupling = coupling_ref[...]
    sum_low, sum_high = flux[0:8], flux[8:12]
    for f in range(state.shape[0]):
        row = state[f : f + 1, :]
        sum_low = sum_low + coupling[0:8, f : f + 1] * row
        sum_high = sum_high + coupling[8:12, f : f + 1] * row
    coupled = jnp.concatenate([sum_low, sum_high, sum_high], axis=0).astype(BF16)
    coupled_wide = coupled.astype(F32)
    half = lax.broadcasted_iota(jnp.int32, (8, 128), 0) // 4
    total_low = jnp.zeros((8, 128), F32)
    total_high = jnp.zeros((8, 128), F32)
    for a in range(blocks):
        area = area_ref[a : a + 1, :]
        total_low = total_low + coupled_wide[0:8, a * 128 : (a + 1) * 128] * area
        total_high = total_high + coupled_wide[8:16, a * 128 : (a + 1) * 128] * area
    total_high = jnp.where(half == 0, total_high, 0.0)
    for a in range(blocks):
        live = count_ref[a]
        part = lax.dot_general(
            coupled[:, a * 128 : (a + 1) * 128],
            weight[a].reshape(links * 128, 128),
            (((1,), (1,)), ((), ())),
            preferred_element_type=F32,
        )
        for link in range(links):
            slot = jnp.where(link < live, slot_ref[a, link], 6 * 3 * subs)
            columns = slice(link * 128, (link + 1) * 128)
            acc_low[slot] += part[0:8, columns]
            acc_high[slot >> 1] += jnp.where(half == (slot & 1), part[8:16, columns], 0.0)
    for p, ref in enumerate((before_out, own_out, after_out)):
        for j in range(subs):
            chunk = p * subs + j
            tiles = [acc_low[chunk * 6 + c] for c in range(6)]
            tiles = tiles + [acc_high[chunk * 3 + c] for c in range(3)]
            packed = jnp.concatenate(tiles, axis=0).astype(BF16)
            ref[j] = packed
            rounded = packed.astype(F32)
            area = arrived[chunk * 8 + 6] + arrived[chunk * 8 + 7]
            for c in range(6):
                total_low = total_low - rounded[c * 8 : c * 8 + 8] * area[c : c + 1]
            for c in range(3):
                both = jnp.where(half == 0, area[2 * c : 2 * c + 1], area[2 * c + 1 : 2 * c + 2])
                total_high = total_high - rounded[48 + c * 8 : 56 + c * 8] * both
    lane = lax.broadcasted_iota(jnp.int32, (8, 128), 1)
    field = lax.broadcasted_iota(jnp.int32, (8, 128), 0)
    low = jnp.where(lane == field, jnp.sum(total_low, axis=1, keepdims=True), 0.0)
    high = jnp.where(lane == 8 + field % 4, jnp.sum(total_high, axis=1, keepdims=True), 0.0)
    row = jnp.sum(low + high, axis=0, keepdims=True)
    total_out[...] = jnp.broadcast_to(row, total_out.shape)


def pack_kernel(total_ref, back_ref, own_ref, ahead_ref, out_ref):
    total = jnp.sum(total_ref[...], axis=0, keepdims=True)
    first = total.astype(BF16).astype(F32)
    second = (total - first).astype(BF16).astype(F32)
    third = total - first - second
    tail = jnp.concatenate([first, second, third, jnp.zeros((5, 128), F32)], axis=0)
    for j in range(out_ref.shape[0]):
        parts = [ref[j].astype(F32) for ref in (back_ref, own_ref, ahead_ref)] + [tail]
        out_ref[j] = jnp.concatenate(parts, axis=0).astype(BF16)


def final_kernel(scale, block_ref, count_ref, in_ref, flux_out, imbalance_out, low, high):
    subs = in_ref.shape[0]
    blocks = flux_out.shape[1] // 128
    low[...] = jnp.zeros_like(low)
    high[...] = jnp.zeros_like(high)
    half = lax.broadcasted_iota(jnp.int32, (8, 128), 0) // 4
    total = jnp.zeros((8, 128), F32)
    for k in range(subs):
        part = in_ref[k].astype(F32)
        for o in range(3):
            live = count_ref[o, 0, k]
            for c in range(6):
                b = jnp.where(c < live, block_ref[o * 6 + c, 0, k], blocks)
                low[b] += part[o * 72 + c * 8 : o * 72 + c * 8 + 8]
                start = o * 72 + 48 + (c // 2) * 8
                high[b] += jnp.where(half == c % 2, part[start : start + 8], 0.0)
        total = total + part[216:224]
    for b in range(blocks):
        upper = high[b]
        tile = jnp.concatenate([low[b], upper[0:4] + upper[4:8]], axis=0)
        flux_out[:, b * 128 : (b + 1) * 128] = tile.astype(BF16)
    row = jnp.sum(total, axis=0, keepdims=True) * scale
    imbalance_out[...] = row[:, : imbalance_out.shape[1]]


def shards(
    ocean_state,
    ocean_area,
    atm_flux,
    atm_area,
    coupling,
    remap_weight,
    send_block,
    send_count,
    link_slot,
    link_count,
):
    atm_blocks, links, width = remap_weight.shape[:3]
    ocean_blocks = ocean_state.shape[1] // width
    groups, subs = lax.axis_size("grp"), lax.axis_size("sub")
    forward = [(i, (i + 1) % groups) for i in range(groups)]
    backward = [(target, source) for source, target in forward]
    params = pltpu.CompilerParams(vmem_limit_bytes=LIMIT)
    chosen = send_block.transpose(1, 3, 0, 2).reshape(18, 1, subs)
    counts = send_count.transpose(1, 0, 2)

    routed = pl.pallas_call(
        gather_kernel,
        out_shape=jax.ShapeDtypeStruct((subs, 192, width), BF16),
        in_specs=[SMEM, VMEM, VMEM],
        out_specs=VMEM,
        scratch_shapes=[
            pltpu.VMEM((ocean_blocks, 8, width), F32),
            pltpu.VMEM((ocean_blocks, width), F32),
            pltpu.VMEM((ocean_blocks, width), F32),
            pltpu.VMEM((3 * subs, 16, width), F32),
        ],
        compiler_params=params,
        name="gather_slots",
    )(chosen, ocean_state, ocean_area.reshape(ocean_blocks, width))

    within = lax.all_to_all(routed, "sub", 0, 0, tiled=True)
    after = lax.ppermute(within[:, 0:64], "grp", backward)
    before = lax.ppermute(within[:, 128:192], "grp", forward)

    slots = 18 * subs
    part = jax.ShapeDtypeStruct((subs, 72, width), BF16)
    state_on_atm, part_before, part_own, part_after, totals = pl.pallas_call(
        middle_kernel,
        out_shape=(
            jax.ShapeDtypeStruct((8, atm_blocks * width), BF16),
            part,
            part,
            part,
            jax.ShapeDtypeStruct((groups, width), F32),
        ),
        in_specs=[SMEM, SMEM, VMEM, VMEM, VMEM, VMEM, VMEM, VMEM, ANY],
        out_specs=(VMEM,) * 5,
        scratch_shapes=[
            pltpu.VMEM(remap_weight.shape, BF16),
            pltpu.VMEM((24 * subs, 8, width), F32),
            pltpu.VMEM((atm_blocks, 8, links * width), F32),
            pltpu.VMEM((8, atm_blocks * width), F32),
            pltpu.VMEM((slots + 2, 8, width), F32),
            pltpu.VMEM((slots // 2 + 1, 8, width), F32),
            pltpu.SemaphoreType.DMA((atm_blocks,)),
        ],
        compiler_params=params,
        name="remap_both_ways",
    )(
        link_slot,
        link_count,
        within,
        before,
        after,
        atm_flux,
        atm_area.reshape(atm_blocks, width),
        coupling,
        remap_weight,
    )

    spread = lax.all_to_all(totals, "grp", 0, 0, tiled=True)
    back_after = lax.ppermute(part_before, "grp", backward)
    back_before = lax.ppermute(part_after, "grp", forward)

    packed = pl.pallas_call(
        pack_kernel,
        out_shape=jax.ShapeDtypeStruct((subs, 224, width), BF16),
        in_specs=[VMEM] * 4,
        out_specs=VMEM,
        compiler_params=params,
        name="pack_flux",
    )(spread, back_before, part_own, back_after)
    returned = lax.all_to_all(packed, "sub", 0, 0, tiled=True)

    scale = 1.0 / math.sqrt(groups * subs * atm_blocks * width)
    flux_on_ocean, imbalance = pl.pallas_call(
        functools.partial(final_kernel, scale),
        out_shape=(
            jax.ShapeDtypeStruct((12, ocean_blocks * width), BF16),
            jax.ShapeDtypeStruct((1, 12), F32),
        ),
        in_specs=[SMEM, SMEM, VMEM],
        out_specs=(VMEM, VMEM),
        scratch_shapes=[
            pltpu.VMEM((ocean_blocks + 1, 8, width), F32),
            pltpu.VMEM((ocean_blocks + 1, 8, width), F32),
        ],
        compiler_params=params,
        name="collect_flux",
    )(chosen, counts, returned)
    return (state_on_atm, flux_on_ocean, imbalance.reshape(12))


def solution(mesh):
    placed = (
        P(None, ("grp", "sub")),
        P(("grp", "sub")),
        P(None, ("grp", "sub")),
        P(("grp", "sub")),
        P(),
        P(("grp", "sub"), None, None, None),
        P(("grp", "sub"), None, None, None),
        P(("grp", "sub"), None, None),
        P(("grp", "sub"), None),
        P(("grp", "sub")),
    )
    return jax.shard_map(
        shards,
        mesh=mesh,
        in_specs=placed,
        out_specs=(P(None, ("grp", "sub")), P(None, ("grp", "sub")), P()),
        check_vma=False,
    )
```

```python
import functools
import math

import jax
import jax.numpy as jnp
from jax import lax
from jax.experimental import pallas as pl
from jax.experimental.pallas import tpu as pltpu
from jax.sharding import PartitionSpec as P

F32 = jnp.float32
BF16 = jnp.bfloat16
VMEM = pl.BlockSpec(memory_space=pltpu.VMEM)
HBM = pl.BlockSpec(memory_space=pltpu.HBM)
WHOLE = pltpu.CompilerParams(vmem_limit_bytes=60 * 1024 * 1024)
PART = pltpu.CompilerParams(vmem_limit_bytes=16 * 1024 * 1024)


def gather_kernel(
    block_hbm, state_hbm, area_hbm, back_out, own_out, ahead_out, block, state, area, fields, high, low, rows, sems
):
    subs = own_out.shape[0]
    blocks = area_hbm.shape[0]
    copies = [
        pltpu.make_async_copy(source, target, sems.at[n])
        for n, (source, target) in enumerate(
            ((block_hbm, block), (state_hbm, state), (area_hbm, area))
        )
    ]
    for copy in copies:
        copy.start()
    rows[...] = jnp.zeros_like(rows)
    copies[2].wait()
    upper = area[...].astype(BF16).astype(F32)
    high[...] = upper
    low[...] = area[...] - upper
    copies[1].wait()
    for b in range(blocks):
        fields[b] = state[:, b * 128 : (b + 1) * 128].astype(F32)
    copies[0].wait()
    for o, out_ref in enumerate((back_out, own_out, ahead_out)):
        for k in range(subs):
            for c in range(6):
                b = block[o * 6 + c, 0, k]
                rows[o * subs + k, c : c + 1, :] = high[pl.ds(b, 1), :]
                rows[o * subs + k, 8 + c : 9 + c, :] = low[pl.ds(b, 1), :]
            for c in range(0, 6, 2):
                pair = [fields[block[o * 6 + c + i, 0, k]] for i in range(2)]
                out_ref[k, c * 8 : c * 8 + 16, :] = jnp.concatenate(pair, axis=0).astype(BF16)
            out_ref[k, 48:64, :] = rows[o * subs + k].astype(BF16)


def join_kernel(before_ref, own_ref, after_ref, out_ref):
    out_ref[:, 0:64, :] = before_ref[...]
    out_ref[:, 64:128, :] = own_ref[...]
    out_ref[:, 128:192, :] = after_ref[...]


def middle_kernel(
    slot_hbm,
    count_hbm,
    arrived_ref,
    flux_hbm,
    area_hbm,
    coupling_hbm,
    weight_hbm,
    state_out,
    part_out,
    slot_ref,
    count_ref,
    flux_ref,
    area_ref,
    coupling_ref,
    weight,
    arrived,
    taken,
    state_sum,
    acc_low,
    acc_high,
    weight_sems,
    sems,
):
    blocks, links = weight_hbm.shape[0], weight_hbm.shape[1]
    subs = arrived_ref.shape[0]
    small = [
        pltpu.make_async_copy(source, target, sems.at[n])
        for n, (source, target) in enumerate(
            (
                (slot_hbm, slot_ref),
                (count_hbm, count_ref),
                (flux_hbm, flux_ref),
                (area_hbm, area_ref),
                (coupling_hbm, coupling_ref),
            )
        )
    ]
    copies = [
        pltpu.make_async_copy(weight_hbm.at[a], weight.at[a], weight_sems.at[a])
        for a in range(blocks)
    ]
    for copy in small + copies:
        copy.start()
    for j in range(subs):
        part = arrived_ref[j].astype(F32).reshape(3, 8, 8, 128)
        for p in range(3):
            arrived[(p * subs + j) * 8 : (p * subs + j + 1) * 8] = part[p]
    acc_low[...] = jnp.zeros_like(acc_low)
    acc_high[...] = jnp.zeros_like(acc_high)
    for copy in small:
        copy.wait()
    for a in range(blocks):
        live = count_ref[a]
        for link in range(links):
            slot = slot_ref[a, link]
            chunk = (slot * 171) >> 10
            tile = arrived[chunk * 2 + slot]
            taken[a, :, link * 128 : (link + 1) * 128] = jnp.where(link < live, tile, 0.0)
    for a in range(blocks):
        copies[a].wait()
        state_sum[:, a * 128 : (a + 1) * 128] = jnp.dot(
            taken[a].astype(BF16),
            weight[a].reshape(links * 128, 128),
            preferred_element_type=F32,
        )
    state = state_sum[...]
    state_out[...] = state.astype(BF16)
    flux = flux_ref[...].astype(F32)
    coupling = jnp.transpose(coupling_ref[...])
    sum_low, sum_high = flux[0:8], flux[8:12]
    for f in range(state.shape[0]):
        row = state[f : f + 1, :]
        sum_low = sum_low + coupling[0:8, f : f + 1] * row
        sum_high = sum_high + coupling[8:12, f : f + 1] * row
    coupled = jnp.concatenate([sum_low, sum_high, sum_high], axis=0).astype(BF16)
    coupled_wide = coupled.astype(F32)
    half = lax.broadcasted_iota(jnp.int32, (8, 128), 0) // 4
    total_low = jnp.zeros((8, 128), F32)
    total_high = jnp.zeros((8, 128), F32)
    for a in range(blocks):
        area = area_ref[a : a + 1, :]
        total_low = total_low + coupled_wide[0:8, a * 128 : (a + 1) * 128] * area
        total_high = total_high + coupled_wide[8:16, a * 128 : (a + 1) * 128] * area
    total_high = jnp.where(half == 0, total_high, 0.0)
    for a in range(blocks):
        live = count_ref[a]
        part = lax.dot_general(
            coupled[:, a * 128 : (a + 1) * 128],
            weight[a].reshape(links * 128, 128),
            (((1,), (1,)), ((), ())),
            preferred_element_type=F32,
        )
        for link in range(links):
            slot = jnp.where(link < live, slot_ref[a, link], 6 * 3 * subs)
            columns = slice(link * 128, (link + 1) * 128)
            acc_low[slot] += part[0:8, columns]
            acc_high[slot >> 1] += jnp.where(half == (slot & 1), part[8:16, columns], 0.0)
    packed = []
    for j in range(subs):
        tiles = []
        for p in range(3):
            chunk = p * subs + j
            tiles += [acc_low[chunk * 6 + c] for c in range(6)]
            tiles += [acc_high[chunk * 3 + c] for c in range(3)]
        values = jnp.concatenate(tiles, axis=0).astype(BF16)
        packed.append(values)
        rounded = values.astype(F32)
        for p in range(3):
            chunk = p * subs + j
            area = arrived[chunk * 8 + 6] + arrived[chunk * 8 + 7]
            for c in range(6):
                start = p * 72 + c * 8
                total_low = total_low - rounded[start : start + 8] * area[c : c + 1]
            for c in range(3):
                start = p * 72 + 48 + c * 8
                both = jnp.where(half == 0, area[2 * c : 2 * c + 1], area[2 * c + 1 : 2 * c + 2])
                total_high = total_high - rounded[start : start + 8] * both
    lane = lax.broadcasted_iota(jnp.int32, (8, 128), 1)
    field = lax.broadcasted_iota(jnp.int32, (8, 128), 0)
    total = jnp.where(lane == field, jnp.sum(total_low, axis=1, keepdims=True), 0.0)
    total += jnp.where(lane == 8 + field % 4, jnp.sum(total_high, axis=1, keepdims=True), 0.0)
    total = jnp.sum(total, axis=0, keepdims=True)
    first = total.astype(BF16).astype(F32)
    second = (total - first).astype(BF16).astype(F32)
    third = total - first - second
    tail = jnp.concatenate([first, second, third, jnp.zeros((5, 128), F32)], axis=0)
    for j in range(subs):
        out = jnp.concatenate([packed[j].astype(F32), tail], axis=0)
        part_out[j] = out.astype(BF16)


def split_kernel(in_ref, back_out, own_out, ahead_out, total_out):
    total = jnp.zeros((8, 128), F32)
    for k in range(in_ref.shape[0]):
        part = in_ref[k].astype(F32)
        for p, ref in enumerate((back_out, own_out, ahead_out)):
            ref[k] = part[p * 72 : p * 72 + 72].astype(BF16)
        total = total + part[216:224]
    row = jnp.sum(total, axis=0, keepdims=True)
    total_out[...] = jnp.broadcast_to(row, total_out.shape)


def final_kernel(block_hbm, count_hbm, before_ref, own_ref, after_ref, flux_out, done_out, block, count, low, high, sems):
    subs = own_ref.shape[0]
    blocks = flux_out.shape[1] // 128
    copies = [
        pltpu.make_async_copy(block_hbm, block, sems.at[0]),
        pltpu.make_async_copy(count_hbm, count, sems.at[1]),
    ]
    for copy in copies:
        copy.start()
    low[...] = jnp.zeros_like(low)
    high[...] = jnp.zeros_like(high)
    half = lax.broadcasted_iota(jnp.int32, (8, 128), 0) // 4
    for copy in copies:
        copy.wait()
    for o, ref in enumerate((before_ref, own_ref, after_ref)):
        for k in range(subs):
            part = ref[k].astype(F32)
            live = count[o, 0, k]
            for c in range(6):
                b = jnp.where(c < live, block[o * 6 + c, 0, k], blocks)
                low[b] += part[c * 8 : c * 8 + 8]
                start = 48 + (c // 2) * 8
                high[b] += jnp.where(half == c % 2, part[start : start + 8], 0.0)
    for b in range(blocks):
        upper = high[b]
        tile = jnp.concatenate([low[b], upper[0:4] + upper[4:8]], axis=0)
        flux_out[:, b * 128 : (b + 1) * 128] = tile.astype(BF16)
    done_out[...] = half


def total_kernel(scale, spread_ref, done_ref, imbalance_out):
    row = jnp.sum(spread_ref[...], axis=0, keepdims=True) * scale
    imbalance_out[...] = row[:, : imbalance_out.shape[1]]


def shards(
    ocean_state,
    ocean_area,
    atm_flux,
    atm_area,
    coupling,
    remap_weight,
    send_block,
    send_count,
    link_slot,
    link_count,
):
    atm_blocks, links, width = remap_weight.shape[:3]
    ocean_blocks = ocean_state.shape[1] // width
    groups, subs = lax.axis_size("grp"), lax.axis_size("sub")
    forward = [(i, (i + 1) % groups) for i in range(groups)]
    backward = [(target, source) for source, target in forward]
    chosen = send_block.transpose(1, 3, 0, 2).reshape(18, 1, subs)
    counts = send_count.transpose(1, 0, 2)

    route = jax.ShapeDtypeStruct((subs, 64, width), BF16)
    to_back, own_slots, to_ahead = pl.pallas_call(
        gather_kernel,
        out_shape=(route, route, route),
        in_specs=[HBM, HBM, HBM],
        out_specs=(VMEM,) * 3,
        scratch_shapes=[
            pltpu.SMEM((18, 1, subs), jnp.int32),
            pltpu.VMEM(ocean_state.shape, BF16),
            pltpu.VMEM((ocean_blocks, width), F32),
            pltpu.VMEM((ocean_blocks, 8, width), F32),
            pltpu.VMEM((ocean_blocks, width), F32),
            pltpu.VMEM((ocean_blocks, width), F32),
            pltpu.VMEM((3 * subs, 16, width), F32),
            pltpu.SemaphoreType.DMA((3,)),
        ],
        compiler_params=WHOLE,
        name="gather_slots",
    )(chosen, ocean_state, ocean_area.reshape(ocean_blocks, width))

    after = lax.ppermute(to_back, "grp", backward)
    before = lax.ppermute(to_ahead, "grp", forward)
    joined = pl.pallas_call(
        join_kernel,
        out_shape=jax.ShapeDtypeStruct((subs, 192, width), BF16),
        in_specs=[VMEM] * 3,
        out_specs=VMEM,
        compiler_params=PART,
        name="join_routes",
    )(before, own_slots, after)
    arrived = lax.all_to_all(joined, "sub", 0, 0, tiled=True)

    slots = 18 * subs
    state_on_atm, partial = pl.pallas_call(
        middle_kernel,
        out_shape=(
            jax.ShapeDtypeStruct((8, atm_blocks * width), BF16),
            jax.ShapeDtypeStruct((subs, 224, width), BF16),
        ),
        in_specs=[HBM, HBM, VMEM, HBM, HBM, HBM, HBM],
        out_specs=(VMEM,) * 2,
        scratch_shapes=[
            pltpu.SMEM(link_slot.shape, jnp.int32),
            pltpu.SMEM(link_count.shape, jnp.int32),
            pltpu.VMEM(atm_flux.shape, BF16),
            pltpu.VMEM((atm_blocks, width), F32),
            pltpu.VMEM((8, 12), F32),
            pltpu.VMEM(remap_weight.shape, BF16),
            pltpu.VMEM((24 * subs, 8, width), F32),
            pltpu.VMEM((atm_blocks, 8, links * width), F32),
            pltpu.VMEM((8, atm_blocks * width), F32),
            pltpu.VMEM((slots + 2, 8, width), F32),
            pltpu.VMEM((slots // 2 + 1, 8, width), F32),
            pltpu.SemaphoreType.DMA((atm_blocks,)),
            pltpu.SemaphoreType.DMA((5,)),
        ],
        compiler_params=WHOLE,
        name="remap_both_ways",
    )(
        link_slot,
        link_count,
        arrived,
        atm_flux,
        atm_area.reshape(atm_blocks, width),
        coupling.T,
        remap_weight,
    )

    returned = lax.all_to_all(partial, "sub", 0, 0, tiled=True)
    route = jax.ShapeDtypeStruct((subs, 72, width), BF16)
    to_back, own_flux, to_ahead, totals = pl.pallas_call(
        split_kernel,
        out_shape=(route, route, route, jax.ShapeDtypeStruct((groups, width), F32)),
        in_specs=[VMEM],
        out_specs=(VMEM,) * 4,
        compiler_params=PART,
        name="split_routes",
    )(returned)
    spread = lax.all_to_all(totals, "grp", 0, 0, tiled=True)
    after = lax.ppermute(to_back, "grp", backward)
    before = lax.ppermute(to_ahead, "grp", forward)

    flux_on_ocean, done = pl.pallas_call(
        final_kernel,
        out_shape=(
            jax.ShapeDtypeStruct((12, ocean_blocks * width), BF16),
            jax.ShapeDtypeStruct((8, width), jnp.int32),
        ),
        in_specs=[HBM, HBM, VMEM, VMEM, VMEM],
        out_specs=(VMEM, VMEM),
        scratch_shapes=[
            pltpu.SMEM((18, 1, subs), jnp.int32),
            pltpu.SMEM((3, 1, subs), jnp.int32),
            pltpu.VMEM((ocean_blocks + 1, 8, width), F32),
            pltpu.VMEM((ocean_blocks + 1, 8, width), F32),
            pltpu.SemaphoreType.DMA((2,)),
        ],
        compiler_params=PART,
        cost_estimate=pl.CostEstimate(flops=10**6, bytes_accessed=8 * 10**6, transcendentals=0),
        name="collect_flux",
    )(chosen, counts, before, own_flux, after)
    scale = 1.0 / math.sqrt(groups * subs * atm_blocks * width)
    imbalance = pl.pallas_call(
        functools.partial(total_kernel, scale),
        out_shape=jax.ShapeDtypeStruct((1, 12), F32),
        in_specs=[VMEM, VMEM],
        out_specs=VMEM,
        compiler_params=PART,
        name="total_all",
    )(spread, done)
    return (state_on_atm, flux_on_ocean, imbalance.reshape(12))


def solution(mesh):
    placed = (
        P(None, ("grp", "sub")),
        P(("grp", "sub")),
        P(None, ("grp", "sub")),
        P(("grp", "sub")),
        P(),
        P(("grp", "sub"), None, None, None),
        P(("grp", "sub"), None, None, None),
        P(("grp", "sub"), None, None),
        P(("grp", "sub"), None),
        P(("grp", "sub")),
    )
    return jax.shard_map(
        shards,
        mesh=mesh,
        in_specs=placed,
        out_specs=(P(None, ("grp", "sub")), P(None, ("grp", "sub")), P()),
        check_vma=False,
    )
```

```python
import functools
import math

import jax
import jax.numpy as jnp
from jax import lax
from jax.experimental import pallas as pl
from jax.experimental.pallas import tpu as pltpu
from jax.sharding import PartitionSpec as P

F32 = jnp.float32
BF16 = jnp.bfloat16
VMEM = pl.BlockSpec(memory_space=pltpu.VMEM)
SMEM = pl.BlockSpec(memory_space=pltpu.SMEM)
HBM = pl.BlockSpec(memory_space=pltpu.HBM)
WHOLE = pltpu.CompilerParams(vmem_limit_bytes=60 * 1024 * 1024)
PART = pltpu.CompilerParams(vmem_limit_bytes=16 * 1024 * 1024)


def gather_kernel(offsets, block_hbm, state_hbm, area_hbm, *refs):
    outs, (block, state, area, fields, high, low, rows, sems) = refs[:-8], refs[-8:]
    subs = outs[0].shape[0]
    blocks = area_hbm.shape[0]
    copies = [
        pltpu.make_async_copy(source, target, sems.at[n])
        for n, (source, target) in enumerate(
            ((block_hbm, block), (state_hbm, state), (area_hbm, area))
        )
    ]
    for copy in copies:
        copy.start()
    rows[...] = jnp.zeros_like(rows)
    copies[2].wait()
    upper = area[...].astype(BF16).astype(F32)
    high[...] = upper
    low[...] = area[...] - upper
    copies[1].wait()
    for b in range(blocks):
        fields[b] = state[:, b * 128 : (b + 1) * 128].astype(F32)
    copies[0].wait()
    for n, (o, out_ref) in enumerate(zip(offsets, outs)):
        for k in range(subs):
            for c in range(6):
                b = block[o * 6 + c, 0, k]
                rows[n * subs + k, c : c + 1, :] = high[pl.ds(b, 1), :]
                rows[n * subs + k, 8 + c : 9 + c, :] = low[pl.ds(b, 1), :]
            for c in range(0, 6, 2):
                pair = [fields[block[o * 6 + c + i, 0, k]] for i in range(2)]
                out_ref[k, c * 8 : c * 8 + 16, :] = jnp.concatenate(pair, axis=0).astype(BF16)
            out_ref[k, 48:64, :] = rows[n * subs + k].astype(BF16)


def join_kernel(before_ref, own_ref, after_ref, out_ref):
    out_ref[:, 0:64, :] = before_ref[...]
    out_ref[:, 64:128, :] = own_ref[...]
    out_ref[:, 128:192, :] = after_ref[...]


def middle_kernel(
    slot_ref,
    arrived_ref,
    column_ref,
    weight,
    state_out,
    part_out,
    arrived,
    taken,
    state_sum,
    acc_low,
    acc_high,
):
    blocks, links = weight.shape[0], weight.shape[1]
    subs = arrived_ref.shape[0]
    acc_low[...] = jnp.zeros_like(acc_low)
    acc_high[...] = jnp.zeros_like(acc_high)
    for j in range(subs):
        part = arrived_ref[j].astype(F32).reshape(3, 8, 8, 128)
        for p in range(3):
            arrived[(p * subs + j) * 8 : (p * subs + j + 1) * 8] = part[p]
    for a in range(blocks):
        for link in range(links):
            slot = slot_ref[a, link]
            chunk = (slot * 171) >> 10
            tile = arrived[chunk * 2 + slot]
            taken[a, :, link * 128 : (link + 1) * 128] = tile
    for a in range(blocks):
        state_sum[:, a * 128 : (a + 1) * 128] = jnp.dot(
            taken[a].astype(BF16),
            weight[a].reshape(links * 128, 128),
            preferred_element_type=F32,
        )
    state = state_sum[...]
    state_out[...] = state.astype(BF16)
    flux = column_ref[0:12, 0 : blocks * 128]
    coupling = column_ref[0:12, blocks * 128 : blocks * 128 + 128]
    sum_low, sum_high = flux[0:8], flux[8:12]
    for f in range(state.shape[0]):
        row = state[f : f + 1, :]
        sum_low = sum_low + coupling[0:8, f : f + 1] * row
        sum_high = sum_high + coupling[8:12, f : f + 1] * row
    coupled = jnp.concatenate([sum_low, sum_high, sum_high], axis=0).astype(BF16)
    coupled_wide = coupled.astype(F32)
    half = lax.broadcasted_iota(jnp.int32, (8, 128), 0) // 4
    total_low = jnp.zeros((8, 128), F32)
    total_high = jnp.zeros((8, 128), F32)
    for a in range(blocks):
        area = column_ref[12:13, a * 128 : (a + 1) * 128]
        total_low = total_low + coupled_wide[0:8, a * 128 : (a + 1) * 128] * area
        total_high = total_high + coupled_wide[8:16, a * 128 : (a + 1) * 128] * area
    total_high = jnp.where(half == 0, total_high, 0.0)
    for a in range(blocks):
        part = lax.dot_general(
            coupled[:, a * 128 : (a + 1) * 128],
            weight[a].reshape(links * 128, 128),
            (((1,), (1,)), ((), ())),
            preferred_element_type=F32,
        )
        for link in range(links):
            slot = slot_ref[a, link]
            columns = slice(link * 128, (link + 1) * 128)
            acc_low[slot] += part[0:8, columns]
            acc_high[slot >> 1] += jnp.where(half == (slot & 1), part[8:16, columns], 0.0)
    packed = []
    for j in range(subs):
        tiles = []
        for p in range(3):
            chunk = p * subs + j
            tiles += [acc_low[chunk * 6 + c] for c in range(6)]
            tiles += [acc_high[chunk * 3 + c] for c in range(3)]
        values = jnp.concatenate(tiles, axis=0).astype(BF16)
        packed.append(values)
        rounded = values.astype(F32)
        for p in range(3):
            chunk = p * subs + j
            area = arrived[chunk * 8 + 6] + arrived[chunk * 8 + 7]
            for c in range(6):
                start = p * 72 + c * 8
                total_low = total_low - rounded[start : start + 8] * area[c : c + 1]
            for c in range(3):
                start = p * 72 + 48 + c * 8
                both = jnp.where(half == 0, area[2 * c : 2 * c + 1], area[2 * c + 1 : 2 * c + 2])
                total_high = total_high - rounded[start : start + 8] * both
    lane = lax.broadcasted_iota(jnp.int32, (8, 128), 1)
    field = lax.broadcasted_iota(jnp.int32, (8, 128), 0)
    total = jnp.where(lane == field, jnp.sum(total_low, axis=1, keepdims=True), 0.0)
    total += jnp.where(lane == 8 + field % 4, jnp.sum(total_high, axis=1, keepdims=True), 0.0)
    total = jnp.sum(total, axis=0, keepdims=True)
    first = total.astype(BF16).astype(F32)
    second = (total - first).astype(BF16).astype(F32)
    third = total - first - second
    tail = jnp.concatenate([first, second, third, jnp.zeros((5, 128), F32)], axis=0)
    for j in range(subs):
        out = jnp.concatenate([packed[j].astype(F32), tail], axis=0)
        part_out[j] = out.astype(BF16)


def split_kernel(in_ref, back_out, own_out, ahead_out):
    for k in range(in_ref.shape[0]):
        part = in_ref[k].astype(F32)
        for p, ref in enumerate((back_out, own_out, ahead_out)):
            ref[k] = part[p * 72 : p * 72 + 72].astype(BF16)


def group_total_kernel(in_ref, total_out):
    total = jnp.zeros((8, 128), F32)
    for k in range(in_ref.shape[0]):
        total = total + in_ref[k, 208:224, :].astype(F32)[8:16]
    row = jnp.sum(total, axis=0, keepdims=True)
    total_out[...] = jnp.broadcast_to(row, total_out.shape)


def final_kernel(block_hbm, count_hbm, before_ref, own_ref, after_ref, flux_out, done_out, block, count, low, high, sems):
    subs = own_ref.shape[0]
    blocks = flux_out.shape[1] // 128
    copies = [
        pltpu.make_async_copy(block_hbm, block, sems.at[0]),
        pltpu.make_async_copy(count_hbm, count, sems.at[1]),
    ]
    for copy in copies:
        copy.start()
    low[...] = jnp.zeros_like(low)
    high[...] = jnp.zeros_like(high)
    half = lax.broadcasted_iota(jnp.int32, (8, 128), 0) // 4
    for copy in copies:
        copy.wait()
    for o, ref in enumerate((before_ref, own_ref, after_ref)):
        for k in range(subs):
            part = ref[k].astype(F32)
            live = count[o, 0, k]
            for c in range(6):
                b = jnp.where(c < live, block[o * 6 + c, 0, k], blocks)
                low[b] += part[c * 8 : c * 8 + 8]
                start = 48 + (c // 2) * 8
                high[b] += jnp.where(half == c % 2, part[start : start + 8], 0.0)
    for b in range(blocks):
        upper = high[b]
        tile = jnp.concatenate([low[b], upper[0:4] + upper[4:8]], axis=0)
        flux_out[:, b * 128 : (b + 1) * 128] = tile.astype(BF16)
    done_out[...] = half


def total_kernel(scale, spread_ref, done_ref, imbalance_out):
    row = jnp.sum(spread_ref[...], axis=0, keepdims=True) * scale
    imbalance_out[...] = row[:, : imbalance_out.shape[1]]


def shards(
    ocean_state,
    ocean_area,
    atm_flux,
    atm_area,
    coupling,
    remap_weight,
    send_block,
    send_count,
    link_slot,
    link_count,
):
    atm_blocks, links, width = remap_weight.shape[:3]
    ocean_blocks = ocean_state.shape[1] // width
    groups, subs = lax.axis_size("grp"), lax.axis_size("sub")
    forward = [(i, (i + 1) % groups) for i in range(groups)]
    backward = [(target, source) for source, target in forward]
    chosen = send_block.transpose(1, 3, 0, 2).reshape(18, 1, subs)
    counts = send_count.transpose(1, 0, 2)

    route = jax.ShapeDtypeStruct((subs, 64, width), BF16)

    def gather(offsets, params):
        return pl.pallas_call(
            functools.partial(gather_kernel, offsets),
            out_shape=(route,) * len(offsets),
            in_specs=[HBM, HBM, HBM],
            out_specs=(VMEM,) * len(offsets),
            scratch_shapes=[
                pltpu.SMEM((18, 1, subs), jnp.int32),
                pltpu.VMEM(ocean_state.shape, BF16),
                pltpu.VMEM((ocean_blocks, width), F32),
                pltpu.VMEM((ocean_blocks, 8, width), F32),
                pltpu.VMEM((ocean_blocks, width), F32),
                pltpu.VMEM((ocean_blocks, width), F32),
                pltpu.VMEM((len(offsets) * subs, 16, width), F32),
                pltpu.SemaphoreType.DMA((3,)),
            ],
            compiler_params=params,
            cost_estimate=pl.CostEstimate(flops=10**6, bytes_accessed=10**6, transcendentals=0),
            name="gather_slots",
        )(chosen, ocean_state, ocean_area.reshape(ocean_blocks, width))

    to_back, to_ahead = gather((0, 2), WHOLE)
    (own_slots,) = gather((1,), PART)
    after = lax.ppermute(to_back, "grp", backward)
    before = lax.ppermute(to_ahead, "grp", forward)
    joined = pl.pallas_call(
        join_kernel,
        out_shape=jax.ShapeDtypeStruct((subs, 192, width), BF16),
        in_specs=[VMEM] * 3,
        out_specs=VMEM,
        compiler_params=PART,
        name="join_routes",
    )(before, own_slots, after)
    arrived = lax.all_to_all(joined, "sub", 0, 0, tiled=True)

    live = lax.broadcasted_iota(jnp.int32, link_slot.shape, 1) < link_count[:, None]
    weight = jnp.where(live[:, :, None, None], remap_weight, jnp.zeros((), BF16))
    columns = jnp.concatenate(
        [
            jnp.concatenate([atm_flux.astype(F32), atm_area[None], jnp.zeros((3, atm_area.shape[0]), F32)], axis=0),
            jnp.pad(coupling, ((0, 4), (0, width - coupling.shape[1]))),
        ],
        axis=1,
    )

    slots = 18 * subs
    state_on_atm, partial = pl.pallas_call(
        middle_kernel,
        out_shape=(
            jax.ShapeDtypeStruct((8, atm_blocks * width), BF16),
            jax.ShapeDtypeStruct((subs, 224, width), BF16),
        ),
        in_specs=[SMEM] + [VMEM] * 3,
        out_specs=(VMEM, VMEM),
        scratch_shapes=[
            pltpu.VMEM((24 * subs, 8, width), F32),
            pltpu.VMEM((atm_blocks, 8, links * width), F32),
            pltpu.VMEM((8, atm_blocks * width), F32),
            pltpu.VMEM((slots, 8, width), F32),
            pltpu.VMEM((slots // 2, 8, width), F32),
        ],
        compiler_params=PART,
        name="remap_both_ways",
    )(
        link_slot,
        arrived,
        columns,
        weight,
    )

    returned = lax.all_to_all(partial, "sub", 0, 0, tiled=True)
    route = jax.ShapeDtypeStruct((subs, 72, width), BF16)
    totals = pl.pallas_call(
        group_total_kernel,
        out_shape=jax.ShapeDtypeStruct((groups, width), F32),
        in_specs=[VMEM],
        out_specs=VMEM,
        compiler_params=PART,
        name="total_group",
    )(returned)
    to_back, own_flux, to_ahead = pl.pallas_call(
        split_kernel,
        out_shape=(route, route, route),
        in_specs=[VMEM],
        out_specs=(VMEM,) * 3,
        compiler_params=PART,
        name="split_routes",
    )(returned)
    spread = lax.all_to_all(totals, "grp", 0, 0, tiled=True)
    after = lax.ppermute(to_back, "grp", backward)
    before = lax.ppermute(to_ahead, "grp", forward)

    flux_on_ocean, done = pl.pallas_call(
        final_kernel,
        out_shape=(
            jax.ShapeDtypeStruct((12, ocean_blocks * width), BF16),
            jax.ShapeDtypeStruct((8, width), jnp.int32),
        ),
        in_specs=[HBM, HBM, VMEM, VMEM, VMEM],
        out_specs=(VMEM, VMEM),
        scratch_shapes=[
            pltpu.SMEM((18, 1, subs), jnp.int32),
            pltpu.SMEM((3, 1, subs), jnp.int32),
            pltpu.VMEM((ocean_blocks + 1, 8, width), F32),
            pltpu.VMEM((ocean_blocks + 1, 8, width), F32),
            pltpu.SemaphoreType.DMA((2,)),
        ],
        compiler_params=PART,
        cost_estimate=pl.CostEstimate(flops=10**6, bytes_accessed=8 * 10**6, transcendentals=0),
        name="collect_flux",
    )(chosen, counts, before, own_flux, after)
    scale = 1.0 / math.sqrt(groups * subs * atm_blocks * width)
    imbalance = pl.pallas_call(
        functools.partial(total_kernel, scale),
        out_shape=jax.ShapeDtypeStruct((1, 12), F32),
        in_specs=[VMEM, VMEM],
        out_specs=VMEM,
        compiler_params=PART,
        name="total_all",
    )(spread, done)
    return (state_on_atm, flux_on_ocean, imbalance.reshape(12))


def solution(mesh):
    placed = (
        P(None, ("grp", "sub")),
        P(("grp", "sub")),
        P(None, ("grp", "sub")),
        P(("grp", "sub")),
        P(),
        P(("grp", "sub"), None, None, None),
        P(("grp", "sub"), None, None, None),
        P(("grp", "sub"), None, None),
        P(("grp", "sub"), None),
        P(("grp", "sub")),
    )
    return jax.shard_map(
        shards,
        mesh=mesh,
        in_specs=placed,
        out_specs=(P(None, ("grp", "sub")), P(None, ("grp", "sub")), P()),
        check_vma=False,
    )
```

```python
import functools
import math

import jax
import jax.numpy as jnp
from jax import lax
from jax.experimental import pallas as pl
from jax.experimental.pallas import tpu as pltpu
from jax.sharding import PartitionSpec as P

F32 = jnp.float32
BF16 = jnp.bfloat16
VMEM = pl.BlockSpec(memory_space=pltpu.VMEM)
SMEM = pl.BlockSpec(memory_space=pltpu.SMEM)
HBM = pl.BlockSpec(memory_space=pltpu.HBM)
WHOLE = pltpu.CompilerParams(vmem_limit_bytes=60 * 1024 * 1024)
PART = pltpu.CompilerParams(vmem_limit_bytes=16 * 1024 * 1024)


def gather_kernel(offsets, block_hbm, state_hbm, area_hbm, *refs):
    outs, (block, state, area, fields, high, low, rows, sems) = refs[:-8], refs[-8:]
    subs = outs[0].shape[0]
    blocks = area_hbm.shape[0]
    copies = [
        pltpu.make_async_copy(source, target, sems.at[n])
        for n, (source, target) in enumerate(
            ((block_hbm, block), (state_hbm, state), (area_hbm, area))
        )
    ]
    for copy in copies:
        copy.start()
    rows[...] = jnp.zeros_like(rows)
    copies[2].wait()
    upper = area[...].astype(BF16).astype(F32)
    high[...] = upper
    low[...] = area[...] - upper
    copies[1].wait()
    for b in range(blocks):
        fields[b] = state[:, b * 128 : (b + 1) * 128].astype(F32)
    copies[0].wait()
    for n, (o, out_ref) in enumerate(zip(offsets, outs)):
        for k in range(subs):
            for c in range(6):
                b = block[o * 6 + c, 0, k]
                rows[n * subs + k, c : c + 1, :] = high[pl.ds(b, 1), :]
                rows[n * subs + k, 8 + c : 9 + c, :] = low[pl.ds(b, 1), :]
            for c in range(0, 6, 2):
                pair = [fields[block[o * 6 + c + i, 0, k]] for i in range(2)]
                out_ref[k, c * 8 : c * 8 + 16, :] = jnp.concatenate(pair, axis=0).astype(BF16)
            out_ref[k, 48:64, :] = rows[n * subs + k].astype(BF16)


def join_kernel(before_ref, own_ref, after_ref, out_ref):
    out_ref[:, 0:64, :] = before_ref[...]
    out_ref[:, 64:128, :] = own_ref[...]
    out_ref[:, 128:192, :] = after_ref[...]


def middle_kernel(
    slot_ref,
    arrived_ref,
    column_ref,
    weight,
    state_out,
    part_out,
    arrived,
    taken,
    state_sum,
    acc_low,
    acc_high,
):
    blocks, links = weight.shape[0], weight.shape[1]
    subs = arrived_ref.shape[0]
    acc_low[...] = jnp.zeros_like(acc_low)
    acc_high[...] = jnp.zeros_like(acc_high)
    for j in range(subs):
        part = arrived_ref[j].astype(F32).reshape(3, 8, 8, 128)
        for p in range(3):
            arrived[(p * subs + j) * 8 : (p * subs + j + 1) * 8] = part[p]
    for a in range(blocks):
        for link in range(links):
            slot = slot_ref[a, link]
            chunk = (slot * 171) >> 10
            tile = arrived[chunk * 2 + slot]
            taken[a, :, link * 128 : (link + 1) * 128] = tile
    for a in range(blocks):
        state_sum[:, a * 128 : (a + 1) * 128] = jnp.dot(
            taken[a].astype(BF16),
            weight[a].reshape(links * 128, 128),
            preferred_element_type=F32,
        )
    state = state_sum[...]
    state_out[...] = state.astype(BF16)
    flux = column_ref[0:12, 0 : blocks * 128]
    coupling = column_ref[0:12, blocks * 128 : blocks * 128 + 128]
    sum_low, sum_high = flux[0:8], flux[8:12]
    for f in range(state.shape[0]):
        row = state[f : f + 1, :]
        sum_low = sum_low + coupling[0:8, f : f + 1] * row
        sum_high = sum_high + coupling[8:12, f : f + 1] * row
    coupled = jnp.concatenate([sum_low, sum_high, sum_high], axis=0).astype(BF16)
    coupled_wide = coupled.astype(F32)
    half = lax.broadcasted_iota(jnp.int32, (8, 128), 0) // 4
    total_low = jnp.zeros((8, 128), F32)
    total_high = jnp.zeros((8, 128), F32)
    for a in range(blocks):
        area = column_ref[12:13, a * 128 : (a + 1) * 128]
        total_low = total_low + coupled_wide[0:8, a * 128 : (a + 1) * 128] * area
        total_high = total_high + coupled_wide[8:16, a * 128 : (a + 1) * 128] * area
    total_high = jnp.where(half == 0, total_high, 0.0)
    for a in range(blocks):
        part = lax.dot_general(
            coupled[:, a * 128 : (a + 1) * 128],
            weight[a].reshape(links * 128, 128),
            (((1,), (1,)), ((), ())),
            preferred_element_type=F32,
        )
        for link in range(links):
            slot = slot_ref[a, link]
            columns = slice(link * 128, (link + 1) * 128)
            acc_low[slot] += part[0:8, columns]
            acc_high[slot >> 1] += jnp.where(half == (slot & 1), part[8:16, columns], 0.0)
    packed = []
    for j in range(subs):
        tiles = []
        for p in range(3):
            chunk = p * subs + j
            tiles += [acc_low[chunk * 6 + c] for c in range(6)]
            tiles += [acc_high[chunk * 3 + c] for c in range(3)]
        values = jnp.concatenate(tiles, axis=0).astype(BF16)
        packed.append(values)
        rounded = values.astype(F32)
        for p in range(3):
            chunk = p * subs + j
            area = arrived[chunk * 8 + 6] + arrived[chunk * 8 + 7]
            for c in range(6):
                start = p * 72 + c * 8
                total_low = total_low - rounded[start : start + 8] * area[c : c + 1]
            for c in range(3):
                start = p * 72 + 48 + c * 8
                both = jnp.where(half == 0, area[2 * c : 2 * c + 1], area[2 * c + 1 : 2 * c + 2])
                total_high = total_high - rounded[start : start + 8] * both
    lane = lax.broadcasted_iota(jnp.int32, (8, 128), 1)
    field = lax.broadcasted_iota(jnp.int32, (8, 128), 0)
    total = jnp.where(lane == field, jnp.sum(total_low, axis=1, keepdims=True), 0.0)
    total += jnp.where(lane == 8 + field % 4, jnp.sum(total_high, axis=1, keepdims=True), 0.0)
    total = jnp.sum(total, axis=0, keepdims=True)
    first = total.astype(BF16).astype(F32)
    second = (total - first).astype(BF16).astype(F32)
    third = total - first - second
    tail = jnp.concatenate([first, second, third, jnp.zeros((5, 128), F32)], axis=0)
    for j in range(subs):
        out = jnp.concatenate([packed[j].astype(F32), tail], axis=0)
        part_out[j] = out.astype(BF16)


def split_kernel(in_ref, back_out, own_out, ahead_out):
    for k in range(in_ref.shape[0]):
        part = in_ref[k].astype(F32)
        for p, ref in enumerate((back_out, own_out, ahead_out)):
            ref[k] = part[p * 72 : p * 72 + 72].astype(BF16)


def group_total_kernel(in_ref, total_out):
    total = jnp.zeros((8, 128), F32)
    for k in range(in_ref.shape[0]):
        total = total + in_ref[k, 208:224, :].astype(F32)[8:16]
    row = jnp.sum(total, axis=0, keepdims=True)
    spare = lax.broadcasted_iota(jnp.int32, total_out.shape, 0) % 2
    total_out[...] = jnp.where(spare == 0, row, 0.0)


def add_slots(o, ref, block, count, low, high):
    half = lax.broadcasted_iota(jnp.int32, (8, 128), 0) // 4
    for k in range(ref.shape[0]):
        part = ref[k].astype(F32)
        live = count[o, 0, k]
        for c in range(6):
            b = jnp.where(c < live, block[o * 6 + c, 0, k], low.shape[0] - 1)
            low[b] += part[c * 8 : c * 8 + 8]
            start = 48 + (c // 2) * 8
            high[b] += jnp.where(half == c % 2, part[start : start + 8], 0.0)


def own_kernel(block, count, own_ref, low, high):
    low[...] = jnp.zeros_like(low)
    high[...] = jnp.zeros_like(high)
    add_slots(1, own_ref, block, count, low, high)


def final_kernel(block, count, before_ref, after_ref, own_low, own_high, flux_out, done_out, low, high):
    blocks = flux_out.shape[1] // 128
    low[...] = own_low[...]
    high[...] = own_high[...]
    add_slots(0, before_ref, block, count, low, high)
    add_slots(2, after_ref, block, count, low, high)
    for b in range(blocks):
        upper = high[b]
        tile = jnp.concatenate([low[b], upper[0:4] + upper[4:8]], axis=0)
        flux_out[:, b * 128 : (b + 1) * 128] = tile.astype(BF16)
    done_out[...] = jnp.zeros_like(done_out)


def total_kernel(scale, spread_ref, done_ref, imbalance_out):
    row = jnp.sum(spread_ref[...], axis=0, keepdims=True) * scale
    imbalance_out[...] = row[:, : imbalance_out.shape[1]]


def shards(
    ocean_state,
    ocean_area,
    atm_flux,
    atm_area,
    coupling,
    remap_weight,
    send_block,
    send_count,
    link_slot,
    link_count,
):
    atm_blocks, links, width = remap_weight.shape[:3]
    ocean_blocks = ocean_state.shape[1] // width
    groups, subs = lax.axis_size("grp"), lax.axis_size("sub")
    forward = [(i, (i + 1) % groups) for i in range(groups)]
    backward = [(target, source) for source, target in forward]
    chosen = send_block.transpose(1, 3, 0, 2).reshape(18, 1, subs)
    counts = send_count.transpose(1, 0, 2)

    route = jax.ShapeDtypeStruct((subs, 64, width), BF16)

    def gather(offsets, params):
        return pl.pallas_call(
            functools.partial(gather_kernel, offsets),
            out_shape=(route,) * len(offsets),
            in_specs=[HBM, HBM, HBM],
            out_specs=(VMEM,) * len(offsets),
            scratch_shapes=[
                pltpu.SMEM((18, 1, subs), jnp.int32),
                pltpu.VMEM(ocean_state.shape, BF16),
                pltpu.VMEM((ocean_blocks, width), F32),
                pltpu.VMEM((ocean_blocks, 8, width), F32),
                pltpu.VMEM((ocean_blocks, width), F32),
                pltpu.VMEM((ocean_blocks, width), F32),
                pltpu.VMEM((len(offsets) * subs, 16, width), F32),
                pltpu.SemaphoreType.DMA((3,)),
            ],
            compiler_params=params,
            cost_estimate=pl.CostEstimate(flops=10**6, bytes_accessed=10**6, transcendentals=0),
            name="gather_slots",
        )(chosen, ocean_state, ocean_area.reshape(ocean_blocks, width))

    to_back, to_ahead = gather((0, 2), WHOLE)
    (own_slots,) = gather((1,), PART)
    after = lax.ppermute(to_back, "grp", backward)
    before = lax.ppermute(to_ahead, "grp", forward)
    joined = pl.pallas_call(
        join_kernel,
        out_shape=jax.ShapeDtypeStruct((subs, 192, width), BF16),
        in_specs=[VMEM] * 3,
        out_specs=VMEM,
        compiler_params=PART,
        name="join_routes",
    )(before, own_slots, after)
    arrived = lax.all_to_all(joined, "sub", 0, 0, tiled=True)

    live = lax.broadcasted_iota(jnp.int32, link_slot.shape, 1) < link_count[:, None]
    weight = jnp.where(live[:, :, None, None], remap_weight, jnp.zeros((), BF16))
    columns = jnp.concatenate(
        [
            jnp.concatenate([atm_flux.astype(F32), atm_area[None], jnp.zeros((3, atm_area.shape[0]), F32)], axis=0),
            jnp.pad(coupling, ((0, 4), (0, width - coupling.shape[1]))),
        ],
        axis=1,
    )

    slots = 18 * subs
    state_on_atm, partial = pl.pallas_call(
        middle_kernel,
        out_shape=(
            jax.ShapeDtypeStruct((8, atm_blocks * width), BF16),
            jax.ShapeDtypeStruct((subs, 224, width), BF16),
        ),
        in_specs=[SMEM] + [VMEM] * 3,
        out_specs=(VMEM, VMEM),
        scratch_shapes=[
            pltpu.VMEM((24 * subs, 8, width), F32),
            pltpu.VMEM((atm_blocks, 8, links * width), F32),
            pltpu.VMEM((8, atm_blocks * width), F32),
            pltpu.VMEM((slots, 8, width), F32),
            pltpu.VMEM((slots // 2, 8, width), F32),
        ],
        compiler_params=PART,
        name="remap_both_ways",
    )(
        link_slot,
        arrived,
        columns,
        weight,
    )

    returned = lax.all_to_all(partial, "sub", 0, 0, tiled=True)
    route = jax.ShapeDtypeStruct((subs, 72, width), BF16)
    totals = pl.pallas_call(
        group_total_kernel,
        out_shape=jax.ShapeDtypeStruct((2 * groups, width), F32),
        in_specs=[VMEM],
        out_specs=VMEM,
        compiler_params=PART,
        name="total_group",
    )(returned)
    to_back, own_flux, to_ahead = pl.pallas_call(
        split_kernel,
        out_shape=(route, route, route),
        in_specs=[VMEM],
        out_specs=(VMEM,) * 3,
        compiler_params=PART,
        name="split_routes",
    )(returned)
    spread = lax.all_to_all(totals, "grp", 0, 0, tiled=True)
    after = lax.ppermute(to_back, "grp", backward)
    before = lax.ppermute(to_ahead, "grp", forward)

    sums = jax.ShapeDtypeStruct((ocean_blocks + 1, 8, width), F32)
    own_low, own_high = pl.pallas_call(
        own_kernel,
        out_shape=(sums, sums),
        in_specs=[SMEM, SMEM, VMEM],
        out_specs=(VMEM, VMEM),
        compiler_params=PART,
        cost_estimate=pl.CostEstimate(flops=10**6, bytes_accessed=8 * 10**6, transcendentals=0),
        name="collect_own",
    )(chosen, counts, own_flux)
    flux_on_ocean, done = pl.pallas_call(
        final_kernel,
        out_shape=(
            jax.ShapeDtypeStruct((12, ocean_blocks * width), BF16),
            jax.ShapeDtypeStruct((8, width), jnp.int32),
        ),
        in_specs=[SMEM, SMEM, VMEM, VMEM, VMEM, VMEM],
        out_specs=(VMEM, VMEM),
        scratch_shapes=[
            pltpu.VMEM(sums.shape, F32),
            pltpu.VMEM(sums.shape, F32),
        ],
        compiler_params=PART,
        cost_estimate=pl.CostEstimate(flops=10**6, bytes_accessed=8 * 10**6, transcendentals=0),
        name="collect_flux",
    )(chosen, counts, before, after, own_low, own_high)
    scale = 1.0 / math.sqrt(groups * subs * atm_blocks * width)
    imbalance = pl.pallas_call(
        functools.partial(total_kernel, scale),
        out_shape=jax.ShapeDtypeStruct((1, 12), F32),
        in_specs=[VMEM, VMEM],
        out_specs=VMEM,
        compiler_params=PART,
        name="total_all",
    )(spread, done)
    return (state_on_atm, flux_on_ocean, imbalance.reshape(12))


def solution(mesh):
    placed = (
        P(None, ("grp", "sub")),
        P(("grp", "sub")),
        P(None, ("grp", "sub")),
        P(("grp", "sub")),
        P(),
        P(("grp", "sub"), None, None, None),
        P(("grp", "sub"), None, None, None),
        P(("grp", "sub"), None, None),
        P(("grp", "sub"), None),
        P(("grp", "sub")),
    )
    return jax.shard_map(
        shards,
        mesh=mesh,
        in_specs=placed,
        out_specs=(P(None, ("grp", "sub")), P(None, ("grp", "sub")), P()),
        check_vma=False,
    )
```

```python
import functools
import math

import jax
import jax.numpy as jnp
from jax import lax
from jax.experimental import pallas as pl
from jax.experimental.pallas import tpu as pltpu
from jax.sharding import PartitionSpec as P

F32 = jnp.float32
BF16 = jnp.bfloat16
VMEM = pl.BlockSpec(memory_space=pltpu.VMEM)
SMEM = pl.BlockSpec(memory_space=pltpu.SMEM)
HBM = pl.BlockSpec(memory_space=pltpu.HBM)
WHOLE = pltpu.CompilerParams(vmem_limit_bytes=60 * 1024 * 1024)
PART = pltpu.CompilerParams(vmem_limit_bytes=16 * 1024 * 1024)


def gather_kernel(block_hbm, state_hbm, area_hbm, out_ref, block, state, area, fields, high, low, rows, sems):
    subs = out_ref.shape[0]
    blocks = area_hbm.shape[0]
    copies = [
        pltpu.make_async_copy(source, target, sems.at[n])
        for n, (source, target) in enumerate(
            ((block_hbm, block), (state_hbm, state), (area_hbm, area))
        )
    ]
    for copy in copies:
        copy.start()
    rows[...] = jnp.zeros_like(rows)
    copies[2].wait()
    upper = area[...].astype(BF16).astype(F32)
    high[...] = upper
    low[...] = area[...] - upper
    copies[1].wait()
    for b in range(blocks):
        fields[b] = state[:, b * 128 : (b + 1) * 128].astype(F32)
    copies[0].wait()
    for o in range(3):
        for k in range(subs):
            for c in range(6):
                b = block[o * 6 + c, 0, k]
                rows[o * subs + k, c : c + 1, :] = high[pl.ds(b, 1), :]
                rows[o * subs + k, 8 + c : 9 + c, :] = low[pl.ds(b, 1), :]
            for c in range(0, 6, 2):
                pair = [fields[block[o * 6 + c + i, 0, k]] for i in range(2)]
                start = o * 64 + c * 8
                out_ref[k, start : start + 16, :] = jnp.concatenate(pair, axis=0).astype(BF16)
            out_ref[k, o * 64 + 48 : o * 64 + 64, :] = rows[o * subs + k].astype(BF16)


def forward_kernel(in_ref, back_out, ahead_out):
    back_out[...] = in_ref[:, 0:64, :]
    ahead_out[...] = in_ref[:, 128:192, :]


def middle_kernel(
    slot_ref,
    within_ref,
    before_ref,
    after_ref,
    column_ref,
    weight,
    state_out,
    part_out,
    arrived,
    taken,
    state_sum,
    acc_low,
    acc_high,
):
    blocks, links = weight.shape[0], weight.shape[1]
    subs = within_ref.shape[0]
    acc_low[...] = jnp.zeros_like(acc_low)
    acc_high[...] = jnp.zeros_like(acc_high)
    for j in range(subs):
        for p, part in enumerate((before_ref[j], within_ref[j, 64:128, :], after_ref[j])):
            tiles = part.astype(F32).reshape(8, 8, 128)
            arrived[(p * subs + j) * 8 : (p * subs + j + 1) * 8] = tiles
    for a in range(blocks):
        for link in range(links):
            slot = slot_ref[a, link]
            chunk = (slot * 171) >> 10
            tile = arrived[chunk * 2 + slot]
            taken[a, :, link * 128 : (link + 1) * 128] = tile
    for a in range(blocks):
        state_sum[:, a * 128 : (a + 1) * 128] = jnp.dot(
            taken[a].astype(BF16),
            weight[a].reshape(links * 128, 128),
            preferred_element_type=F32,
        )
    state = state_sum[...]
    state_out[...] = state.astype(BF16)
    flux = column_ref[0:12, 0 : blocks * 128]
    coupling = column_ref[0:12, blocks * 128 : blocks * 128 + 128]
    sum_low, sum_high = flux[0:8], flux[8:12]
    for f in range(state.shape[0]):
        row = state[f : f + 1, :]
        sum_low = sum_low + coupling[0:8, f : f + 1] * row
        sum_high = sum_high + coupling[8:12, f : f + 1] * row
    coupled = jnp.concatenate([sum_low, sum_high, sum_high], axis=0).astype(BF16)
    coupled_wide = coupled.astype(F32)
    half = lax.broadcasted_iota(jnp.int32, (8, 128), 0) // 4
    total_low = jnp.zeros((8, 128), F32)
    total_high = jnp.zeros((8, 128), F32)
    for a in range(blocks):
        area = column_ref[12:13, a * 128 : (a + 1) * 128]
        total_low = total_low + coupled_wide[0:8, a * 128 : (a + 1) * 128] * area
        total_high = total_high + coupled_wide[8:16, a * 128 : (a + 1) * 128] * area
    total_high = jnp.where(half == 0, total_high, 0.0)
    for a in range(blocks):
        part = lax.dot_general(
            coupled[:, a * 128 : (a + 1) * 128],
            weight[a].reshape(links * 128, 128),
            (((1,), (1,)), ((), ())),
            preferred_element_type=F32,
        )
        for link in range(links):
            slot = slot_ref[a, link]
            columns = slice(link * 128, (link + 1) * 128)
            acc_low[slot] += part[0:8, columns]
            acc_high[slot >> 1] += jnp.where(half == (slot & 1), part[8:16, columns], 0.0)
    packed = []
    for j in range(subs):
        tiles = []
        for p in range(3):
            chunk = p * subs + j
            tiles += [acc_low[chunk * 6 + c] for c in range(6)]
            tiles += [acc_high[chunk * 3 + c] for c in range(3)]
        values = jnp.concatenate(tiles, axis=0).astype(BF16)
        packed.append(values)
        rounded = values.astype(F32)
        for p in range(3):
            chunk = p * subs + j
            area = arrived[chunk * 8 + 6] + arrived[chunk * 8 + 7]
            for c in range(6):
                start = p * 72 + c * 8
                total_low = total_low - rounded[start : start + 8] * area[c : c + 1]
            for c in range(3):
                start = p * 72 + 48 + c * 8
                both = jnp.where(half == 0, area[2 * c : 2 * c + 1], area[2 * c + 1 : 2 * c + 2])
                total_high = total_high - rounded[start : start + 8] * both
    lane = lax.broadcasted_iota(jnp.int32, (8, 128), 1)
    field = lax.broadcasted_iota(jnp.int32, (8, 128), 0)
    total = jnp.where(lane == field, jnp.sum(total_low, axis=1, keepdims=True), 0.0)
    total += jnp.where(lane == 8 + field % 4, jnp.sum(total_high, axis=1, keepdims=True), 0.0)
    total = jnp.sum(total, axis=0, keepdims=True)
    first = total.astype(BF16).astype(F32)
    second = (total - first).astype(BF16).astype(F32)
    third = total - first - second
    tail = jnp.concatenate([first, second, third, jnp.zeros((5, 128), F32)], axis=0)
    for j in range(subs):
        out = jnp.concatenate([packed[j].astype(F32), tail], axis=0)
        part_out[j] = out.astype(BF16)


def split_kernel(in_ref, back_out, own_out, ahead_out):
    for k in range(in_ref.shape[0]):
        part = in_ref[k].astype(F32)
        for p, ref in enumerate((back_out, own_out, ahead_out)):
            ref[k] = part[p * 72 : p * 72 + 72].astype(BF16)


def group_total_kernel(in_ref, total_out):
    total = jnp.zeros((8, 128), F32)
    for k in range(in_ref.shape[0]):
        total = total + in_ref[k, 208:224, :].astype(F32)[8:16]
    row = jnp.sum(total, axis=0, keepdims=True)
    spare = lax.broadcasted_iota(jnp.int32, total_out.shape, 0) % 2
    total_out[...] = jnp.where(spare == 0, row, 0.0)


def add_slots(offsets, refs, block, count, lows, highs):
    half = lax.broadcasted_iota(jnp.int32, (8, 128), 0) // 4
    for k in range(refs[0].shape[0]):
        parts = [ref[k].astype(F32) for ref in refs]
        for c in range(6):
            for o, part, low, high in zip(offsets, parts, lows, highs):
                b = jnp.where(c < count[o, 0, k], block[o * 6 + c, 0, k], low.shape[0] - 1)
                low[b] += part[c * 8 : c * 8 + 8]
                start = 48 + (c // 2) * 8
                high[b] += jnp.where(half == c % 2, part[start : start + 8], 0.0)


def own_kernel(block, count, own_ref, low, high):
    low[...] = jnp.zeros_like(low)
    high[...] = jnp.zeros_like(high)
    add_slots((1,), (own_ref,), block, count, (low,), (high,))


def final_kernel(block, count, before_ref, after_ref, own_low, own_high, flux_out, done_out, low, high, more_low, more_high):
    blocks = flux_out.shape[1] // 128
    for ref in (low, high, more_low, more_high):
        ref[...] = jnp.zeros_like(ref)
    add_slots(
        (0, 2), (before_ref, after_ref), block, count, (low, more_low), (high, more_high)
    )
    for b in range(blocks):
        upper = high[b] + more_high[b] + own_high[b]
        lower = low[b] + more_low[b] + own_low[b]
        tile = jnp.concatenate([lower, upper[0:4] + upper[4:8]], axis=0)
        flux_out[:, b * 128 : (b + 1) * 128] = tile.astype(BF16)
    done_out[...] = jnp.zeros_like(done_out)


def total_kernel(scale, spread_ref, done_ref, imbalance_out):
    row = jnp.sum(spread_ref[...], axis=0, keepdims=True) * scale
    imbalance_out[...] = row[:, : imbalance_out.shape[1]]


def shards(
    ocean_state,
    ocean_area,
    atm_flux,
    atm_area,
    coupling,
    remap_weight,
    send_block,
    send_count,
    link_slot,
    link_count,
):
    atm_blocks, links, width = remap_weight.shape[:3]
    ocean_blocks = ocean_state.shape[1] // width
    groups, subs = lax.axis_size("grp"), lax.axis_size("sub")
    forward = [(i, (i + 1) % groups) for i in range(groups)]
    backward = [(target, source) for source, target in forward]
    chosen = send_block.transpose(1, 3, 0, 2).reshape(18, 1, subs)
    counts = send_count.transpose(1, 0, 2)

    routed = pl.pallas_call(
        gather_kernel,
        out_shape=jax.ShapeDtypeStruct((subs, 192, width), BF16),
        in_specs=[HBM, HBM, HBM],
        out_specs=VMEM,
        scratch_shapes=[
            pltpu.SMEM((18, 1, subs), jnp.int32),
            pltpu.VMEM(ocean_state.shape, BF16),
            pltpu.VMEM((ocean_blocks, width), F32),
            pltpu.VMEM((ocean_blocks, 8, width), F32),
            pltpu.VMEM((ocean_blocks, width), F32),
            pltpu.VMEM((ocean_blocks, width), F32),
            pltpu.VMEM((3 * subs, 16, width), F32),
            pltpu.SemaphoreType.DMA((3,)),
        ],
        compiler_params=WHOLE,
        name="gather_slots",
    )(chosen, ocean_state, ocean_area.reshape(ocean_blocks, width))
    within = lax.all_to_all(routed, "sub", 0, 0, tiled=True)
    route = jax.ShapeDtypeStruct((subs, 64, width), BF16)
    to_back, to_ahead = pl.pallas_call(
        forward_kernel,
        out_shape=(route, route),
        in_specs=[VMEM],
        out_specs=(VMEM, VMEM),
        compiler_params=PART,
        name="forward_routes",
    )(within)
    after = lax.ppermute(to_back, "grp", backward)
    before = lax.ppermute(to_ahead, "grp", forward)

    live = lax.broadcasted_iota(jnp.int32, link_slot.shape, 1) < link_count[:, None]
    weight = jnp.where(live[:, :, None, None], remap_weight, jnp.zeros((), BF16))
    columns = jnp.concatenate(
        [
            jnp.concatenate([atm_flux.astype(F32), atm_area[None], jnp.zeros((3, atm_area.shape[0]), F32)], axis=0),
            jnp.pad(coupling, ((0, 4), (0, width - coupling.shape[1]))),
        ],
        axis=1,
    )

    slots = 18 * subs
    state_on_atm, partial = pl.pallas_call(
        middle_kernel,
        out_shape=(
            jax.ShapeDtypeStruct((8, atm_blocks * width), BF16),
            jax.ShapeDtypeStruct((subs, 224, width), BF16),
        ),
        in_specs=[SMEM] + [VMEM] * 5,
        out_specs=(VMEM, VMEM),
        scratch_shapes=[
            pltpu.VMEM((24 * subs, 8, width), F32),
            pltpu.VMEM((atm_blocks, 8, links * width), F32),
            pltpu.VMEM((8, atm_blocks * width), F32),
            pltpu.VMEM((slots, 8, width), F32),
            pltpu.VMEM((slots // 2, 8, width), F32),
        ],
        compiler_params=PART,
        name="remap_both_ways",
    )(
        link_slot,
        within,
        before,
        after,
        columns,
        weight,
    )

    returned = lax.all_to_all(partial, "sub", 0, 0, tiled=True)
    route = jax.ShapeDtypeStruct((subs, 72, width), BF16)
    totals = pl.pallas_call(
        group_total_kernel,
        out_shape=jax.ShapeDtypeStruct((2 * groups, width), F32),
        in_specs=[VMEM],
        out_specs=VMEM,
        compiler_params=PART,
        name="total_group",
    )(returned)
    to_back, own_flux, to_ahead = pl.pallas_call(
        split_kernel,
        out_shape=(route, route, route),
        in_specs=[VMEM],
        out_specs=(VMEM,) * 3,
        compiler_params=PART,
        name="split_routes",
    )(returned)
    spread = lax.all_to_all(totals, "grp", 0, 0, tiled=True)
    after = lax.ppermute(to_back, "grp", backward)
    before = lax.ppermute(to_ahead, "grp", forward)

    sums = jax.ShapeDtypeStruct((ocean_blocks + 1, 8, width), F32)
    own_low, own_high = pl.pallas_call(
        own_kernel,
        out_shape=(sums, sums),
        in_specs=[SMEM, SMEM, VMEM],
        out_specs=(VMEM, VMEM),
        compiler_params=PART,
        cost_estimate=pl.CostEstimate(flops=10**6, bytes_accessed=8 * 10**6, transcendentals=0),
        name="collect_own",
    )(chosen, counts, own_flux)
    flux_on_ocean, done = pl.pallas_call(
        final_kernel,
        out_shape=(
            jax.ShapeDtypeStruct((12, ocean_blocks * width), BF16),
            jax.ShapeDtypeStruct((8, width), jnp.int32),
        ),
        in_specs=[SMEM, SMEM, VMEM, VMEM, VMEM, VMEM],
        out_specs=(VMEM, VMEM),
        scratch_shapes=[
            pltpu.VMEM(sums.shape, F32),
            pltpu.VMEM(sums.shape, F32),
            pltpu.VMEM(sums.shape, F32),
            pltpu.VMEM(sums.shape, F32),
        ],
        compiler_params=PART,
        cost_estimate=pl.CostEstimate(flops=10**6, bytes_accessed=8 * 10**6, transcendentals=0),
        name="collect_flux",
    )(chosen, counts, before, after, own_low, own_high)
    scale = 1.0 / math.sqrt(groups * subs * atm_blocks * width)
    imbalance = pl.pallas_call(
        functools.partial(total_kernel, scale),
        out_shape=jax.ShapeDtypeStruct((1, 12), F32),
        in_specs=[VMEM, VMEM],
        out_specs=VMEM,
        compiler_params=PART,
        name="total_all",
    )(spread, done)
    return (state_on_atm, flux_on_ocean, imbalance.reshape(12))


def solution(mesh):
    placed = (
        P(None, ("grp", "sub")),
        P(("grp", "sub")),
        P(None, ("grp", "sub")),
        P(("grp", "sub")),
        P(),
        P(("grp", "sub"), None, None, None),
        P(("grp", "sub"), None, None, None),
        P(("grp", "sub"), None, None),
        P(("grp", "sub"), None),
        P(("grp", "sub")),
    )
    return jax.shard_map(
        shards,
        mesh=mesh,
        in_specs=placed,
        out_specs=(P(None, ("grp", "sub")), P(None, ("grp", "sub")), P()),
        check_vma=False,
    )
```

```python
import functools
import math

import jax
import jax.numpy as jnp
from jax import lax
from jax.experimental import pallas as pl
from jax.experimental.pallas import tpu as pltpu
from jax.sharding import PartitionSpec as P

F32 = jnp.float32
BF16 = jnp.bfloat16
VMEM = pl.BlockSpec(memory_space=pltpu.VMEM)
SMEM = pl.BlockSpec(memory_space=pltpu.SMEM)
HBM = pl.BlockSpec(memory_space=pltpu.HBM)
WHOLE = pltpu.CompilerParams(vmem_limit_bytes=60 * 1024 * 1024)
PART = pltpu.CompilerParams(vmem_limit_bytes=16 * 1024 * 1024)


def gather_kernel(block_hbm, state_hbm, area_hbm, out_ref, block, state, area, fields, high, low, rows, sems):
    subs = out_ref.shape[0]
    blocks = area_hbm.shape[0]
    copies = [
        pltpu.make_async_copy(source, target, sems.at[n])
        for n, (source, target) in enumerate(
            ((block_hbm, block), (state_hbm, state), (area_hbm, area))
        )
    ]
    for copy in copies:
        copy.start()
    rows[...] = jnp.zeros_like(rows)
    copies[2].wait()
    upper = area[...].astype(BF16).astype(F32)
    high[...] = upper
    low[...] = area[...] - upper
    copies[1].wait()
    for b in range(blocks):
        fields[b] = state[:, b * 128 : (b + 1) * 128].astype(F32)
    copies[0].wait()
    for o in range(3):
        for k in range(subs):
            for c in range(6):
                b = block[o * 6 + c, 0, k]
                rows[o * subs + k, c : c + 1, :] = high[pl.ds(b, 1), :]
                rows[o * subs + k, 8 + c : 9 + c, :] = low[pl.ds(b, 1), :]
            for c in range(0, 6, 2):
                pair = [fields[block[o * 6 + c + i, 0, k]] for i in range(2)]
                start = o * 64 + c * 8
                out_ref[k, start : start + 16, :] = jnp.concatenate(pair, axis=0).astype(BF16)
            out_ref[k, o * 64 + 48 : o * 64 + 64, :] = rows[o * subs + k].astype(BF16)


def forward_kernel(in_ref, chip_out, core_out):
    start = pl.multiple_of(lax.axis_index("grp") % 2 * 128, 128)
    chip_out[...] = in_ref[:, pl.ds(start, 64), :]
    core_out[...] = in_ref[:, pl.ds(128 - start, 64), :]


def middle_kernel(
    slot_ref,
    within_ref,
    chip_ref,
    core_ref,
    column_ref,
    weight,
    state_out,
    part_out,
    arrived,
    taken,
    state_sum,
    acc_low,
    acc_high,
):
    blocks, links = weight.shape[0], weight.shape[1]
    subs = within_ref.shape[0]
    far = lax.axis_index("grp") % 2 * 2
    acc_low[...] = jnp.zeros_like(acc_low)
    acc_high[...] = jnp.zeros_like(acc_high)
    for j in range(subs):
        for p, part in ((far, chip_ref[j]), (1, within_ref[j, 64:128, :]), (2 - far, core_ref[j])):
            tiles = part.astype(F32).reshape(8, 8, 128)
            arrived[pl.ds((p * subs + j) * 8, 8)] = tiles
    for a in range(blocks):
        for link in range(links):
            slot = slot_ref[a, link]
            chunk = (slot * 171) >> 10
            tile = arrived[chunk * 2 + slot]
            taken[a, :, link * 128 : (link + 1) * 128] = tile
    for a in range(blocks):
        state_sum[:, a * 128 : (a + 1) * 128] = jnp.dot(
            taken[a].astype(BF16),
            weight[a].reshape(links * 128, 128),
            preferred_element_type=F32,
        )
    state = state_sum[...]
    state_out[...] = state.astype(BF16)
    flux = column_ref[0:12, 0 : blocks * 128]
    coupling = column_ref[0:12, blocks * 128 : blocks * 128 + 128]
    sum_low, sum_high = flux[0:8], flux[8:12]
    for f in range(state.shape[0]):
        row = state[f : f + 1, :]
        sum_low = sum_low + coupling[0:8, f : f + 1] * row
        sum_high = sum_high + coupling[8:12, f : f + 1] * row
    coupled = jnp.concatenate([sum_low, sum_high, sum_high], axis=0).astype(BF16)
    coupled_wide = coupled.astype(F32)
    half = lax.broadcasted_iota(jnp.int32, (8, 128), 0) // 4
    total_low = jnp.zeros((8, 128), F32)
    total_high = jnp.zeros((8, 128), F32)
    for a in range(blocks):
        area = column_ref[12:13, a * 128 : (a + 1) * 128]
        total_low = total_low + coupled_wide[0:8, a * 128 : (a + 1) * 128] * area
        total_high = total_high + coupled_wide[8:16, a * 128 : (a + 1) * 128] * area
    total_high = jnp.where(half == 0, total_high, 0.0)
    for a in range(blocks):
        part = lax.dot_general(
            coupled[:, a * 128 : (a + 1) * 128],
            weight[a].reshape(links * 128, 128),
            (((1,), (1,)), ((), ())),
            preferred_element_type=F32,
        )
        for link in range(links):
            slot = slot_ref[a, link]
            columns = slice(link * 128, (link + 1) * 128)
            acc_low[slot] += part[0:8, columns]
            acc_high[slot >> 1] += jnp.where(half == (slot & 1), part[8:16, columns], 0.0)
    packed = []
    for j in range(subs):
        tiles = []
        for p in range(3):
            chunk = p * subs + j
            tiles += [acc_low[chunk * 6 + c] for c in range(6)]
            tiles += [acc_high[chunk * 3 + c] for c in range(3)]
        values = jnp.concatenate(tiles, axis=0).astype(BF16)
        packed.append(values)
        rounded = values.astype(F32)
        for p in range(3):
            chunk = p * subs + j
            area = arrived[chunk * 8 + 6] + arrived[chunk * 8 + 7]
            for c in range(6):
                start = p * 72 + c * 8
                total_low = total_low - rounded[start : start + 8] * area[c : c + 1]
            for c in range(3):
                start = p * 72 + 48 + c * 8
                both = jnp.where(half == 0, area[2 * c : 2 * c + 1], area[2 * c + 1 : 2 * c + 2])
                total_high = total_high - rounded[start : start + 8] * both
    lane = lax.broadcasted_iota(jnp.int32, (8, 128), 1)
    field = lax.broadcasted_iota(jnp.int32, (8, 128), 0)
    total = jnp.where(lane == field, jnp.sum(total_low, axis=1, keepdims=True), 0.0)
    total += jnp.where(lane == 8 + field % 4, jnp.sum(total_high, axis=1, keepdims=True), 0.0)
    total = jnp.sum(total, axis=0, keepdims=True)
    first = total.astype(BF16).astype(F32)
    second = (total - first).astype(BF16).astype(F32)
    third = total - first - second
    tail = jnp.concatenate([first, second, third, jnp.zeros((5, 128), F32)], axis=0)
    for j in range(subs):
        out = jnp.concatenate([packed[j].astype(F32), tail], axis=0)
        part_out[j] = out.astype(BF16)


def split_kernel(in_ref, chip_out, own_out, core_out):
    odd = lax.axis_index("grp") % 2 == 1
    for k in range(in_ref.shape[0]):
        part = in_ref[k].astype(F32)
        back, own, ahead = (part[p * 72 : p * 72 + 72] for p in range(3))
        chip_out[k] = jnp.where(odd, ahead, back).astype(BF16)
        own_out[k] = own.astype(BF16)
        core_out[k] = jnp.where(odd, back, ahead).astype(BF16)


def group_total_kernel(in_ref, total_out):
    total = jnp.zeros((8, 128), F32)
    for k in range(in_ref.shape[0]):
        total = total + in_ref[k, 208:224, :].astype(F32)[8:16]
    row = jnp.sum(total, axis=0, keepdims=True)
    spare = lax.broadcasted_iota(jnp.int32, total_out.shape, 0) % 2
    total_out[...] = jnp.where(spare == 0, row, 0.0)


def add_slots(offsets, refs, block, count, lows, highs):
    half = lax.broadcasted_iota(jnp.int32, (8, 128), 0) // 4
    for k in range(refs[0].shape[0]):
        parts = [ref[k].astype(F32) for ref in refs]
        for c in range(6):
            for o, part, low, high in zip(offsets, parts, lows, highs):
                b = jnp.where(c < count[o, 0, k], block[o * 6 + c, 0, k], low.shape[0] - 1)
                low[b] += part[c * 8 : c * 8 + 8]
                start = 48 + (c // 2) * 8
                high[b] += jnp.where(half == c % 2, part[start : start + 8], 0.0)


def own_kernel(block, count, own_ref, low, high):
    low[...] = jnp.zeros_like(low)
    high[...] = jnp.zeros_like(high)
    add_slots((1,), (own_ref,), block, count, (low,), (high,))


def final_kernel(block, count, chip_ref, core_ref, own_low, own_high, flux_out, done_out, low, high, more_low, more_high):
    blocks = flux_out.shape[1] // 128
    for ref in (low, high, more_low, more_high):
        ref[...] = jnp.zeros_like(ref)
    far = lax.axis_index("grp") % 2 * 2
    add_slots(
        (far, 2 - far), (chip_ref, core_ref), block, count, (low, more_low), (high, more_high)
    )
    for b in range(blocks):
        upper = high[b] + more_high[b] + own_high[b]
        lower = low[b] + more_low[b] + own_low[b]
        tile = jnp.concatenate([lower, upper[0:4] + upper[4:8]], axis=0)
        flux_out[:, b * 128 : (b + 1) * 128] = tile.astype(BF16)
    done_out[...] = jnp.zeros_like(done_out)


def total_kernel(scale, spread_ref, done_ref, imbalance_out):
    row = jnp.sum(spread_ref[...], axis=0, keepdims=True) * scale
    imbalance_out[...] = row[:, : imbalance_out.shape[1]]


def shards(
    ocean_state,
    ocean_area,
    atm_flux,
    atm_area,
    coupling,
    remap_weight,
    send_block,
    send_count,
    link_slot,
    link_count,
):
    atm_blocks, links, width = remap_weight.shape[:3]
    ocean_blocks = ocean_state.shape[1] // width
    groups, subs = lax.axis_size("grp"), lax.axis_size("sub")
    across_chips = [(i, (i + 1 if i % 2 else i - 1) % groups) for i in range(groups)]
    across_cores = [(i, i ^ 1) for i in range(groups)]
    chosen = send_block.transpose(1, 3, 0, 2).reshape(18, 1, subs)
    counts = send_count.transpose(1, 0, 2)

    routed = pl.pallas_call(
        gather_kernel,
        out_shape=jax.ShapeDtypeStruct((subs, 192, width), BF16),
        in_specs=[HBM, HBM, HBM],
        out_specs=VMEM,
        scratch_shapes=[
            pltpu.SMEM((18, 1, subs), jnp.int32),
            pltpu.VMEM(ocean_state.shape, BF16),
            pltpu.VMEM((ocean_blocks, width), F32),
            pltpu.VMEM((ocean_blocks, 8, width), F32),
            pltpu.VMEM((ocean_blocks, width), F32),
            pltpu.VMEM((ocean_blocks, width), F32),
            pltpu.VMEM((3 * subs, 16, width), F32),
            pltpu.SemaphoreType.DMA((3,)),
        ],
        compiler_params=WHOLE,
        name="gather_slots",
    )(chosen, ocean_state, ocean_area.reshape(ocean_blocks, width))
    within = lax.all_to_all(routed, "sub", 0, 0, tiled=True)
    route = jax.ShapeDtypeStruct((subs, 64, width), BF16)
    to_chip, to_core = pl.pallas_call(
        forward_kernel,
        out_shape=(route, route),
        in_specs=[VMEM],
        out_specs=(VMEM, VMEM),
        compiler_params=PART,
        name="forward_routes",
    )(within)
    from_chip = lax.ppermute(to_chip, "grp", across_chips)
    from_core = lax.ppermute(to_core, "grp", across_cores)

    live = lax.broadcasted_iota(jnp.int32, link_slot.shape, 1) < link_count[:, None]
    weight = jnp.where(live[:, :, None, None], remap_weight, jnp.zeros((), BF16))
    columns = jnp.concatenate(
        [
            jnp.concatenate([atm_flux.astype(F32), atm_area[None], jnp.zeros((3, atm_area.shape[0]), F32)], axis=0),
            jnp.pad(coupling, ((0, 4), (0, width - coupling.shape[1]))),
        ],
        axis=1,
    )

    slots = 18 * subs
    state_on_atm, partial = pl.pallas_call(
        middle_kernel,
        out_shape=(
            jax.ShapeDtypeStruct((8, atm_blocks * width), BF16),
            jax.ShapeDtypeStruct((subs, 224, width), BF16),
        ),
        in_specs=[SMEM] + [VMEM] * 5,
        out_specs=(VMEM, VMEM),
        scratch_shapes=[
            pltpu.VMEM((24 * subs, 8, width), F32),
            pltpu.VMEM((atm_blocks, 8, links * width), F32),
            pltpu.VMEM((8, atm_blocks * width), F32),
            pltpu.VMEM((slots, 8, width), F32),
            pltpu.VMEM((slots // 2, 8, width), F32),
        ],
        compiler_params=PART,
        name="remap_both_ways",
    )(
        link_slot,
        within,
        from_chip,
        from_core,
        columns,
        weight,
    )

    returned = lax.all_to_all(partial, "sub", 0, 0, tiled=True)
    route = jax.ShapeDtypeStruct((subs, 72, width), BF16)
    totals = pl.pallas_call(
        group_total_kernel,
        out_shape=jax.ShapeDtypeStruct((2 * groups, width), F32),
        in_specs=[VMEM],
        out_specs=VMEM,
        compiler_params=PART,
        name="total_group",
    )(returned)
    to_chip, own_flux, to_core = pl.pallas_call(
        split_kernel,
        out_shape=(route, route, route),
        in_specs=[VMEM],
        out_specs=(VMEM,) * 3,
        compiler_params=PART,
        name="split_routes",
    )(returned)
    spread = lax.all_to_all(totals, "grp", 0, 0, tiled=True)
    from_chip = lax.ppermute(to_chip, "grp", across_chips)
    from_core = lax.ppermute(to_core, "grp", across_cores)

    sums = jax.ShapeDtypeStruct((ocean_blocks + 1, 8, width), F32)
    own_low, own_high = pl.pallas_call(
        own_kernel,
        out_shape=(sums, sums),
        in_specs=[SMEM, SMEM, VMEM],
        out_specs=(VMEM, VMEM),
        compiler_params=PART,
        cost_estimate=pl.CostEstimate(flops=10**6, bytes_accessed=8 * 10**6, transcendentals=0),
        name="collect_own",
    )(chosen, counts, own_flux)
    flux_on_ocean, done = pl.pallas_call(
        final_kernel,
        out_shape=(
            jax.ShapeDtypeStruct((12, ocean_blocks * width), BF16),
            jax.ShapeDtypeStruct((8, width), jnp.int32),
        ),
        in_specs=[SMEM, SMEM, VMEM, VMEM, VMEM, VMEM],
        out_specs=(VMEM, VMEM),
        scratch_shapes=[
            pltpu.VMEM(sums.shape, F32),
            pltpu.VMEM(sums.shape, F32),
            pltpu.VMEM(sums.shape, F32),
            pltpu.VMEM(sums.shape, F32),
        ],
        compiler_params=PART,
        cost_estimate=pl.CostEstimate(flops=10**6, bytes_accessed=8 * 10**6, transcendentals=0),
        name="collect_flux",
    )(chosen, counts, from_chip, from_core, own_low, own_high)
    scale = 1.0 / math.sqrt(groups * subs * atm_blocks * width)
    imbalance = pl.pallas_call(
        functools.partial(total_kernel, scale),
        out_shape=jax.ShapeDtypeStruct((1, 12), F32),
        in_specs=[VMEM, VMEM],
        out_specs=VMEM,
        compiler_params=PART,
        name="total_all",
    )(spread, done)
    return (state_on_atm, flux_on_ocean, imbalance.reshape(12))


def solution(mesh):
    placed = (
        P(None, ("grp", "sub")),
        P(("grp", "sub")),
        P(None, ("grp", "sub")),
        P(("grp", "sub")),
        P(),
        P(("grp", "sub"), None, None, None),
        P(("grp", "sub"), None, None, None),
        P(("grp", "sub"), None, None),
        P(("grp", "sub"), None),
        P(("grp", "sub")),
    )
    return jax.shard_map(
        shards,
        mesh=mesh,
        in_specs=placed,
        out_specs=(P(None, ("grp", "sub")), P(None, ("grp", "sub")), P()),
        check_vma=False,
    )
```

```python
import functools
import math

import jax
import jax.numpy as jnp
from jax import lax
from jax.experimental import pallas as pl
from jax.experimental.pallas import tpu as pltpu
from jax.sharding import PartitionSpec as P

F32 = jnp.float32
BF16 = jnp.bfloat16
VMEM = pl.BlockSpec(memory_space=pltpu.VMEM)
SMEM = pl.BlockSpec(memory_space=pltpu.SMEM)
HBM = pl.BlockSpec(memory_space=pltpu.HBM)
WHOLE = pltpu.CompilerParams(vmem_limit_bytes=60 * 1024 * 1024)
PART = pltpu.CompilerParams(vmem_limit_bytes=16 * 1024 * 1024)


def gather_kernel(block_hbm, state_hbm, area_hbm, out_ref, block, state, area, fields, high, low, rows, sems):
    subs = out_ref.shape[0]
    blocks = area_hbm.shape[0]
    copies = [
        pltpu.make_async_copy(source, target, sems.at[n])
        for n, (source, target) in enumerate(
            ((block_hbm, block), (state_hbm, state), (area_hbm, area))
        )
    ]
    for copy in copies:
        copy.start()
    rows[...] = jnp.zeros_like(rows)
    copies[2].wait()
    upper = area[...].astype(BF16).astype(F32)
    high[...] = upper
    low[...] = area[...] - upper
    copies[1].wait()
    for b in range(blocks):
        fields[b] = state[:, b * 128 : (b + 1) * 128].astype(F32)
    copies[0].wait()
    for o in range(3):
        for k in range(subs):
            for c in range(6):
                b = block[o * 6 + c, 0, k]
                rows[o * subs + k, c : c + 1, :] = high[pl.ds(b, 1), :]
                rows[o * subs + k, 8 + c : 9 + c, :] = low[pl.ds(b, 1), :]
            for c in range(0, 6, 2):
                pair = [fields[block[o * 6 + c + i, 0, k]] for i in range(2)]
                start = o * 64 + c * 8
                out_ref[k, start : start + 16, :] = jnp.concatenate(pair, axis=0).astype(BF16)
            out_ref[k, o * 64 + 48 : o * 64 + 64, :] = rows[o * subs + k].astype(BF16)


def forward_kernel(in_ref, chip_out, core_out):
    start = pl.multiple_of(lax.axis_index("grp") % 2 * 128, 128)
    chip_out[...] = in_ref[:, pl.ds(start, 64), :]
    core_out[...] = in_ref[:, pl.ds(128 - start, 64), :]


def middle_kernel(
    slot_ref,
    within_ref,
    chip_ref,
    core_ref,
    column_ref,
    weight,
    state_out,
    part_out,
    arrived,
    taken,
    state_sum,
    acc_low,
    acc_high,
):
    blocks, links = weight.shape[0], weight.shape[1]
    subs = within_ref.shape[0]
    far = lax.axis_index("grp") % 2 * 2
    acc_low[...] = jnp.zeros_like(acc_low)
    acc_high[...] = jnp.zeros_like(acc_high)
    for j in range(subs):
        for p, part in ((far, chip_ref[j]), (1, within_ref[j, 64:128, :]), (2 - far, core_ref[j])):
            tiles = part.astype(F32).reshape(8, 8, 128)
            arrived[pl.ds((p * subs + j) * 8, 8)] = tiles
    for a in range(blocks):
        for link in range(links):
            slot = slot_ref[a, link]
            chunk = (slot * 171) >> 10
            tile = arrived[chunk * 2 + slot]
            taken[a, :, link * 128 : (link + 1) * 128] = tile
    for a in range(blocks):
        state_sum[:, a * 128 : (a + 1) * 128] = jnp.dot(
            taken[a].astype(BF16),
            weight[a].reshape(links * 128, 128),
            preferred_element_type=F32,
        )
    state = state_sum[...]
    state_out[...] = state.astype(BF16)
    flux = column_ref[0:12, 0 : blocks * 128]
    coupling = column_ref[0:12, blocks * 128 : blocks * 128 + 128]
    sum_low, sum_high = flux[0:8], flux[8:12]
    for f in range(state.shape[0]):
        row = state[f : f + 1, :]
        sum_low = sum_low + coupling[0:8, f : f + 1] * row
        sum_high = sum_high + coupling[8:12, f : f + 1] * row
    coupled = jnp.concatenate([sum_low, sum_high, sum_high], axis=0).astype(BF16)
    coupled_wide = coupled.astype(F32)
    half = lax.broadcasted_iota(jnp.int32, (8, 128), 0) // 4
    total_low = jnp.zeros((8, 128), F32)
    total_high = jnp.zeros((8, 128), F32)
    for a in range(blocks):
        area = column_ref[12:13, a * 128 : (a + 1) * 128]
        total_low = total_low + coupled_wide[0:8, a * 128 : (a + 1) * 128] * area
        total_high = total_high + coupled_wide[8:16, a * 128 : (a + 1) * 128] * area
    total_high = jnp.where(half == 0, total_high, 0.0)
    for a in range(blocks):
        part = lax.dot_general(
            coupled[:, a * 128 : (a + 1) * 128],
            weight[a].reshape(links * 128, 128),
            (((1,), (1,)), ((), ())),
            preferred_element_type=F32,
        )
        for link in range(links):
            slot = slot_ref[a, link]
            columns = slice(link * 128, (link + 1) * 128)
            acc_low[slot] += part[0:8, columns]
            acc_high[slot >> 1] += jnp.where(half == (slot & 1), part[8:16, columns], 0.0)
    packed = []
    for j in range(subs):
        tiles = []
        for p in range(3):
            chunk = p * subs + j
            tiles += [acc_low[chunk * 6 + c] for c in range(6)]
            tiles += [acc_high[chunk * 3 + c] for c in range(3)]
        values = jnp.concatenate(tiles, axis=0).astype(BF16)
        packed.append(values)
        rounded = values.astype(F32)
        for p in range(3):
            chunk = p * subs + j
            area = arrived[chunk * 8 + 6] + arrived[chunk * 8 + 7]
            for c in range(6):
                start = p * 72 + c * 8
                total_low = total_low - rounded[start : start + 8] * area[c : c + 1]
            for c in range(3):
                start = p * 72 + 48 + c * 8
                both = jnp.where(half == 0, area[2 * c : 2 * c + 1], area[2 * c + 1 : 2 * c + 2])
                total_high = total_high - rounded[start : start + 8] * both
    lane = lax.broadcasted_iota(jnp.int32, (8, 128), 1)
    field = lax.broadcasted_iota(jnp.int32, (8, 128), 0)
    total = jnp.where(lane == field, jnp.sum(total_low, axis=1, keepdims=True), 0.0)
    total += jnp.where(lane == 8 + field % 4, jnp.sum(total_high, axis=1, keepdims=True), 0.0)
    total = jnp.sum(total, axis=0, keepdims=True)
    first = total.astype(BF16).astype(F32)
    second = (total - first).astype(BF16).astype(F32)
    third = total - first - second
    tail = jnp.concatenate([first, second, third, jnp.zeros((5, 128), F32)], axis=0)
    for j in range(subs):
        out = jnp.concatenate([packed[j].astype(F32), tail], axis=0)
        part_out[j] = out.astype(BF16)


def split_kernel(in_ref, chip_out, own_out, core_out):
    odd = lax.axis_index("grp") % 2 == 1
    for k in range(in_ref.shape[0]):
        part = in_ref[k].astype(F32)
        back, own, ahead = (part[p * 72 : p * 72 + 72] for p in range(3))
        chip_out[k] = jnp.where(odd, ahead, back).astype(BF16)
        own_out[k] = own.astype(BF16)
        core_out[k] = jnp.where(odd, back, ahead).astype(BF16)


def group_total_kernel(in_ref, total_out):
    total = jnp.zeros((8, 128), F32)
    for k in range(in_ref.shape[0]):
        total = total + in_ref[k, 208:224, :].astype(F32)[8:16]
    row = jnp.sum(total, axis=0, keepdims=True)
    spare = lax.broadcasted_iota(jnp.int32, total_out.shape, 0) % 2
    total_out[...] = jnp.where(spare == 0, row, 0.0)


def add_slots(offsets, refs, block, count, lows, highs):
    half = lax.broadcasted_iota(jnp.int32, (8, 128), 0) // 4
    for k in range(refs[0].shape[0]):
        parts = [ref[k].astype(F32) for ref in refs]
        for c in range(6):
            for o, part, low, high in zip(offsets, parts, lows, highs):
                b = jnp.where(c < count[o, 0, k], block[o * 6 + c, 0, k], low.shape[0] - 1)
                low[b] += part[c * 8 : c * 8 + 8]
                start = 48 + (c // 2) * 8
                high[b] += jnp.where(half == c % 2, part[start : start + 8], 0.0)


def own_kernel(block, count, own_ref, low, high):
    low[...] = jnp.zeros_like(low)
    high[...] = jnp.zeros_like(high)
    add_slots((1,), (own_ref,), block, count, (low,), (high,))


def final_kernel(block, count, chip_ref, core_ref, own_low, own_high, flux_out, done_out, low, high, more_low, more_high):
    blocks = flux_out.shape[1] // 128
    for ref in (low, high, more_low, more_high):
        ref[...] = jnp.zeros_like(ref)
    far = lax.axis_index("grp") % 2 * 2
    add_slots(
        (far, 2 - far), (chip_ref, core_ref), block, count, (low, more_low), (high, more_high)
    )
    for b in range(blocks):
        upper = high[b] + more_high[b] + own_high[b]
        lower = low[b] + more_low[b] + own_low[b]
        tile = jnp.concatenate([lower, upper[0:4] + upper[4:8]], axis=0)
        flux_out[:, b * 128 : (b + 1) * 128] = tile.astype(BF16)
    done_out[...] = jnp.zeros_like(done_out)


def total_kernel(scale, spread_ref, done_ref, imbalance_out):
    row = jnp.sum(spread_ref[...], axis=0, keepdims=True) * scale
    imbalance_out[...] = row[:, : imbalance_out.shape[1]]


def shards(
    ocean_state,
    ocean_area,
    atm_flux,
    atm_area,
    coupling,
    remap_weight,
    send_block,
    send_count,
    link_slot,
    link_count,
):
    atm_blocks, links, width = remap_weight.shape[:3]
    ocean_blocks = ocean_state.shape[1] // width
    groups, subs = lax.axis_size("grp"), lax.axis_size("sub")
    across_chips = [(i, (i + 1 if i % 2 else i - 1) % groups) for i in range(groups)]
    across_cores = [(i, i ^ 1) for i in range(groups)]
    chosen = send_block.transpose(1, 3, 0, 2).reshape(18, 1, subs)
    counts = send_count.transpose(1, 0, 2)

    routed = pl.pallas_call(
        gather_kernel,
        out_shape=jax.ShapeDtypeStruct((subs, 192, width), BF16),
        in_specs=[HBM, HBM, HBM],
        out_specs=VMEM,
        scratch_shapes=[
            pltpu.SMEM((18, 1, subs), jnp.int32),
            pltpu.VMEM(ocean_state.shape, BF16),
            pltpu.VMEM((ocean_blocks, width), F32),
            pltpu.VMEM((ocean_blocks, 8, width), F32),
            pltpu.VMEM((ocean_blocks, width), F32),
            pltpu.VMEM((ocean_blocks, width), F32),
            pltpu.VMEM((3 * subs, 16, width), F32),
            pltpu.SemaphoreType.DMA((3,)),
        ],
        compiler_params=WHOLE,
        name="gather_slots",
    )(chosen, ocean_state, ocean_area.reshape(ocean_blocks, width))
    within = lax.all_to_all(routed, "sub", 0, 0, tiled=True)
    route = jax.ShapeDtypeStruct((subs, 64, width), BF16)
    to_chip, to_core = pl.pallas_call(
        forward_kernel,
        out_shape=(route, route),
        in_specs=[VMEM],
        out_specs=(VMEM, VMEM),
        compiler_params=PART,
        name="forward_routes",
    )(within)

    live = lax.broadcasted_iota(jnp.int32, link_slot.shape, 1) < link_count[:, None]
    weight = jnp.where(live[:, :, None, None], remap_weight, jnp.zeros((), BF16))
    flux_wide, to_chip, to_core = lax.optimization_barrier((atm_flux.astype(F32), to_chip, to_core))
    columns = jnp.concatenate(
        [
            jnp.concatenate([flux_wide, atm_area[None], jnp.zeros((3, atm_area.shape[0]), F32)], axis=0),
            jnp.pad(coupling, ((0, 4), (0, width - coupling.shape[1]))),
        ],
        axis=1,
    )

    from_chip = lax.ppermute(to_chip, "grp", across_chips)
    from_core = lax.ppermute(to_core, "grp", across_cores)

    slots = 18 * subs
    state_on_atm, partial = pl.pallas_call(
        middle_kernel,
        out_shape=(
            jax.ShapeDtypeStruct((8, atm_blocks * width), BF16),
            jax.ShapeDtypeStruct((subs, 224, width), BF16),
        ),
        in_specs=[SMEM] + [VMEM] * 5,
        out_specs=(VMEM, VMEM),
        scratch_shapes=[
            pltpu.VMEM((24 * subs, 8, width), F32),
            pltpu.VMEM((atm_blocks, 8, links * width), F32),
            pltpu.VMEM((8, atm_blocks * width), F32),
            pltpu.VMEM((slots, 8, width), F32),
            pltpu.VMEM((slots // 2, 8, width), F32),
        ],
        compiler_params=PART,
        name="remap_both_ways",
    )(
        jnp.where(live, link_slot, 0),
        within,
        from_chip,
        from_core,
        columns,
        weight,
    )

    returned = lax.all_to_all(partial, "sub", 0, 0, tiled=True)
    route = jax.ShapeDtypeStruct((subs, 72, width), BF16)
    totals = pl.pallas_call(
        group_total_kernel,
        out_shape=jax.ShapeDtypeStruct((2 * groups, width), F32),
        in_specs=[VMEM],
        out_specs=VMEM,
        compiler_params=PART,
        name="total_group",
    )(returned)
    to_chip, own_flux, to_core = pl.pallas_call(
        split_kernel,
        out_shape=(route, route, route),
        in_specs=[VMEM],
        out_specs=(VMEM,) * 3,
        compiler_params=PART,
        name="split_routes",
    )(returned)
    spread = lax.all_to_all(totals, "grp", 0, 0, tiled=True)
    from_chip = lax.ppermute(to_chip, "grp", across_chips)
    from_core = lax.ppermute(to_core, "grp", across_cores)

    sums = jax.ShapeDtypeStruct((ocean_blocks + 1, 8, width), F32)
    own_low, own_high = pl.pallas_call(
        own_kernel,
        out_shape=(sums, sums),
        in_specs=[SMEM, SMEM, VMEM],
        out_specs=(VMEM, VMEM),
        compiler_params=PART,
        cost_estimate=pl.CostEstimate(flops=10**6, bytes_accessed=8 * 10**6, transcendentals=0),
        name="collect_own",
    )(chosen, counts, own_flux)
    flux_on_ocean, done = pl.pallas_call(
        final_kernel,
        out_shape=(
            jax.ShapeDtypeStruct((12, ocean_blocks * width), BF16),
            jax.ShapeDtypeStruct((8, width), jnp.int32),
        ),
        in_specs=[SMEM, SMEM, VMEM, VMEM, VMEM, VMEM],
        out_specs=(VMEM, VMEM),
        scratch_shapes=[
            pltpu.VMEM(sums.shape, F32),
            pltpu.VMEM(sums.shape, F32),
            pltpu.VMEM(sums.shape, F32),
            pltpu.VMEM(sums.shape, F32),
        ],
        compiler_params=PART,
        cost_estimate=pl.CostEstimate(flops=10**6, bytes_accessed=8 * 10**6, transcendentals=0),
        name="collect_flux",
    )(chosen, counts, from_chip, from_core, own_low, own_high)
    scale = 1.0 / math.sqrt(groups * subs * atm_blocks * width)
    imbalance = pl.pallas_call(
        functools.partial(total_kernel, scale),
        out_shape=jax.ShapeDtypeStruct((1, 12), F32),
        in_specs=[VMEM, VMEM],
        out_specs=VMEM,
        compiler_params=PART,
        name="total_all",
    )(spread, done)
    return (state_on_atm, flux_on_ocean, imbalance.reshape(12))


def solution(mesh):
    placed = (
        P(None, ("grp", "sub")),
        P(("grp", "sub")),
        P(None, ("grp", "sub")),
        P(("grp", "sub")),
        P(),
        P(("grp", "sub"), None, None, None),
        P(("grp", "sub"), None, None, None),
        P(("grp", "sub"), None, None),
        P(("grp", "sub"), None),
        P(("grp", "sub")),
    )
    return jax.shard_map(
        shards,
        mesh=mesh,
        in_specs=placed,
        out_specs=(P(None, ("grp", "sub")), P(None, ("grp", "sub")), P()),
        check_vma=False,
    )
```
